32 devices in a mesh: gx: 8 (over z, x), gy: 4 (over y, core).
Axes of the slice: x: 2, y: 2, z: 4, core: 2. Of those that a mesh axis runs over, the one named last changes fastest.
Arguments:
- flow_state: float32 [4, 128, 128, 128], P(None, 'gx', 'gy'), may hold values from -10 to 10
- viscosity: float32 [128, 128, 128], P('gx', 'gy'), may hold values from 300 to 1200
Outputs:
- flow_next: float32 [4, 128, 128, 128], P(None, 'gx', 'gy')
The draws below stay inside these ranges and needn't reach their ends.
All inputs are finite; a program needn't handle non-finite values.
Results may differ from the reference program's by a relative error of at most 0.0003.
Values sent between devices are 32-bit elements; how exact they have to be, the bound alone decides.
No kernel may reach another device: no remote copies, remote signals or barrier semaphores. Data moves between devices by JAX's collectives and lax.ppermute only.
A program may use at most 64 MiB of HBM per device.

```python
import math
import jax
import jax.numpy as jnp
from jax import lax

FIELDS = 4
NZ = 128
STEPS = 1
NX = 128
NY = 128


def draw_flow_state(key, part):
    rough_key = jax.random.fold_in(key, 11)
    offset_key = jax.random.fold_in(key, 12)
    phase_key = jax.random.fold_in(key, 14)
    amplitude_key = jax.random.fold_in(key, 15)
    rough_part = jax.random.truncated_normal(rough_key, -3.0, 3.0, (FIELDS, NX, NY, NZ), jnp.float32)
    x_angle = jnp.arange(NX, dtype=jnp.float32).reshape(1, NX, 1, 1) * (2.0 * math.pi / NX)
    y_angle = jnp.arange(NY, dtype=jnp.float32).reshape(1, 1, NY, 1) * (2.0 * math.pi / NY)
    phases = jax.random.uniform(phase_key, (2, FIELDS, 1, 1, 1), jnp.float32, -math.pi, math.pi)
    offset = jax.random.uniform(offset_key, (FIELDS, 1, 1, 1), jnp.float32, -1.5, 1.5)
    amplitudes = jax.random.uniform(amplitude_key, (2, FIELDS, 1, 1, 1), jnp.float32, 1.5, 2.0)
    trend = amplitudes[0] * jnp.cos(x_angle + phases[0]) + amplitudes[1] * jnp.cos(y_angle + phases[1])
    return rough_part + offset + trend


def steps_of(stream_key, dims, pieces, least, high):
    factor_of = 1.0
    for dim, blocks in pieces:
        steps = jax.random.uniform(jax.random.fold_in(jax.random.fold_in(stream_key, 6), dim), (blocks,), jnp.float32, least / len(pieces), high / len(pieces))
        factor_of = factor_of * jnp.repeat(jnp.exp(steps), dims[dim] // blocks).reshape((-1,) + (1,) * (len(dims) - 1 - dim))
    return factor_of


def setup_inputs(seed: int = 0) -> dict:
    streams_of = jax.random.split(jax.random.key(seed), 3)
    flow_state = draw_flow_state(jax.random.fold_in(streams_of[2], 71), 0)
    viscosity = jnp.clip(jnp.exp(math.log(1200.0) - 1.3862944 * jax.random.uniform(streams_of[1], (NX, NY, NZ), jnp.float32) ** steps_of(streams_of[1], (NX, NY, NZ), ((0, 8), (1, 4)), -0.2, 0.2)), 300.0, 1200.0)
    return dict(flow_state=flow_state, viscosity=viscosity)


ADVECT = 0.2
BUOYANT = 0.5
CONDUCT = 0.6

def advect(flow_state):
    padded = jnp.pad(flow_state, ((0, 0), (1, 1), (1, 1), (0, 0)))
    along_x = 0.5 * (padded[:, 2:, 1:-1] - padded[:, :-2, 1:-1])
    along_y = 0.5 * (padded[:, 1:-1, 2:] - padded[:, 1:-1, :-2])
    along_z = 0.5 * (jnp.roll(flow_state, -1, 3) - jnp.roll(flow_state, 1, 3))
    carried = flow_state[0:1] * along_x + flow_state[1:2] * along_y + flow_state[2:3] * along_z
    source = flow_state - ADVECT * carried
    return jnp.concatenate([source[:2], source[2:3] + BUOYANT * flow_state[3:4], source[3:]], 0)

def solve_line(field, coefficient, along):
    moved = jnp.moveaxis(field, along, -1)
    spread = jnp.moveaxis(coefficient, along, -1)
    face_values = jnp.concatenate([spread[..., :1], 0.5 * (spread[..., :-1] + spread[..., 1:]), spread[..., -1:]], -1)
    length = moved.shape[-1]
    position = lax.broadcasted_iota(jnp.int32, moved.shape, moved.ndim - 1)
    lowers = jnp.where(position == 0, 0.0, -face_values[..., :-1])
    uppers = jnp.where(position == length - 1, 0.0, -face_values[..., 1:])
    middle = 1.0 + face_values[..., :-1] + face_values[..., 1:]
    solution = lax.linalg.tridiagonal_solve(lowers, middle, uppers, moved[..., None])[..., 0]
    return jnp.moveaxis(solution, -1, along)

def reference(flow_state, viscosity):
    coefficients = [viscosity, viscosity, viscosity, CONDUCT * viscosity]
    current = flow_state
    for repeat in range(STEPS):
        source = advect(current)
        fields = [solve_line(source[i], coefficients[i], 0) for i in range(4)]
        fields = [solve_line(fields[i], coefficients[i], 1) for i in range(4)]
        current = jnp.stack(fields)
    return current
```

```python
import functools

import jax
import jax.numpy as jnp
from jax import lax
from jax.experimental import pallas as pl
from jax.experimental.pallas import tpu as pltpu
from jax.sharding import PartitionSpec as P

ADVECT = 0.2
BUOYANT = 0.5
CONDUCT = 0.6
GROUPS = (0, 0, 0, 1)
SCALES = (1.0, CONDUCT)
VMEM = pl.BlockSpec(memory_space=pltpu.VMEM)
ANY = pl.BlockSpec(memory_space=pl.ANY)
F32 = jnp.float32


def call(kernel, ins, outs, scratch=(), in_specs=None, cost=1000000):
    return pl.pallas_call(
        kernel,
        out_shape=[jax.ShapeDtypeStruct(shape, F32) for shape in outs],
        in_specs=in_specs or [VMEM] * len(ins),
        out_specs=[VMEM] * len(outs),
        scratch_shapes=list(scratch),
        compiler_params=pltpu.CompilerParams(vmem_limit_bytes=40 * 1024 * 1024),
        cost_estimate=pl.CostEstimate(flops=cost, bytes_accessed=cost, transcendentals=0),
    )(*ins)


def pick(flag, a, b):
    return jnp.where(flag, a, b)


def pack_kernel(flow, visc, x_even, x_odd, y_even, y_odd, sems):
    nx, ny = flow.shape[1], flow.shape[2]
    x_par = lax.rem(lax.axis_index("gx"), 2)
    y_par = lax.rem(lax.axis_index("gy"), 2)
    copies = []
    for out, row in ((x_even, (1 - x_par) * (nx - 1)), (x_odd, x_par * (nx - 1))):
        copies.append((flow.at[:, row], out.at[pl.ds(0, 4)]))
        copies.append((visc.at[row], out.at[4]))
    for out, row in ((y_even, (1 - y_par) * (ny - 1)), (y_odd, y_par * (ny - 1))):
        copies.append((flow.at[:, :, row], out.at[pl.ds(0, 4)]))
        copies.append((visc.at[:, row], out.at[4]))
    started = [pltpu.make_async_copy(a, b, sems.at[i]) for i, (a, b) in enumerate(copies)]
    for copy in started:
        copy.start()
    for copy in started:
        copy.wait()


def factor_line(load, count, first, last, inv, ratio, left, right):
    for group, scale in enumerate(SCALES):
        here = load(0)
        excess = 1.0 + pick(first, scale * here, 0.0)
        column = None
        columns = []
        for i in range(count):
            if i < count - 1:
                beyond = load(i + 1)
                face = (0.5 * scale) * (here + beyond)
                inverse = 1.0 / (excess + face)
                portion = face * inverse
                ratio[group, i] = portion
                inv[group, i] = inverse
                columns.append(column)
                column = portion if column is None else column * portion
                excess = 1.0 + portion * excess
                here = beyond
            else:
                excess = excess + pick(last, scale * here, 0.0)
                inverse = 1.0 / excess
                inv[group, i] = inverse
                ratio[group, i] = inverse
                columns.append(column)
        response = inverse
        onward = column * inverse
        right[group, count - 1] = response
        left[group, count - 1] = onward
        for i in range(count - 2, -1, -1):
            portion = ratio[group, i]
            response = portion * response
            start = inv[group, i] if i == 0 else columns[i] * inv[group, i]
            onward = start + portion * onward
            right[group, i] = response
            left[group, i] = onward


def factor_kernel(visc, ivx, rx, cx, wx, ivy, ry, cy, wy):
    nx, ny, nz = visc.shape
    ix, iy = lax.axis_index("gx"), lax.axis_index("gy")
    mx, my = lax.axis_size("gx"), lax.axis_size("gy")
    factor_line(lambda i: visc[i], nx, ix == 0, ix == mx - 1, ivx, rx, cx, wx)
    rows = visc.reshape(nx * ny, nz)
    factor_line(
        lambda j: rows[pl.ds(j, nx, stride=ny), :], ny, iy == 0, iy == my - 1, ivy, ry, cy, wy
    )


def source_kernel(flow, visc, x_even, x_odd, y_even, y_odd, cx, wx, source, message):
    _, nx, ny, nz = flow.shape
    x_par = lax.rem(lax.axis_index("gx"), 2) == 0
    y_par = lax.rem(lax.axis_index("gy"), 2) == 0
    row = lax.broadcasted_iota(jnp.int32, (ny, nz), 0)
    left = [None] * 4
    right = [None] * 4
    for i in range(nx):
        velocity = [ADVECT * 0.5 * flow[c, i] for c in range(3)]
        temperature = None
        for c in (3, 0, 1, 2):
            f = flow[c, i]
            if i == 0:
                down = pick(x_par, x_odd[c], x_even[c])
            else:
                down = flow[c, i - 1]
            if i == nx - 1:
                up = pick(x_par, x_even[c], x_odd[c])
            else:
                up = flow[c, i + 1]
            y_low = pick(y_par, y_odd[c, pl.ds(i, 1)], y_even[c, pl.ds(i, 1)])
            y_high = pick(y_par, y_even[c, pl.ds(i, 1)], y_odd[c, pl.ds(i, 1)])
            below = pick(row == 0, y_low, pltpu.roll(f, 1, 0))
            above = pick(row == ny - 1, y_high, pltpu.roll(f, ny - 1, 0))
            z_low = pltpu.roll(f, 1, 1)
            z_high = pltpu.roll(f, nz - 1, 1)
            s = f - (
                velocity[0] * (up - down)
                + velocity[1] * (above - below)
                + velocity[2] * (z_high - z_low)
            )
            if c == 3:
                temperature = f
            if c == 2:
                s = s + BUOYANT * temperature
            source[c, i] = s
            group = GROUPS[c]
            a, b = cx[group, i] * s, wx[group, i] * s
            left[c] = a if i == 0 else left[c] + a
            right[c] = b if i == 0 else right[c] + b
    for c in range(4):
        message[c] = left[c]
        message[4 + c] = right[c]
    beyond = pick(x_par, x_even[4], x_odd[4])
    face = 0.5 * (visc[nx - 1] + beyond)
    for group, scale in enumerate(SCALES):
        message[8 + group] = cx[group, 0]
        message[10 + group] = cx[group, nx - 1]
        message[12 + group] = wx[group, nx - 1] + 1.0 / (scale * face)


def merge_kernel(axis, bit, last, mine, theirs, union, saved):
    is_left = (lax.axis_index(axis) & bit) == 0
    next_left = (lax.axis_index(axis) & (2 * bit)) == 0

    def a(k):
        return pick(is_left, mine[k], theirs[k])

    def b(k):
        return pick(is_left, theirs[k], mine[k])

    for group in range(2):
        a_lr, b_lr = a(10 + group), b(10 + group)
        m = 1.0 / (a(12 + group) + b(8 + group))
        pa, pb = m * a_lr, m * b_lr
        saved[4 + group] = pa
        saved[6 + group] = pb
        out_ll = a(8 + group) - a_lr * pa
        out_rr = b(12 + group) - b_lr * pb
        if last:
            union[4 + group] = pick(next_left, out_rr, out_ll)
        else:
            union[8 + group] = out_ll
            union[10 + group] = a_lr * pb
            union[12 + group] = out_rr
        for c in range(4):
            if GROUPS[c] != group:
                continue
            d = b(c) - a(4 + c)
            saved[c] = m * d
            out_l = a(c) + pa * d
            out_r = b(4 + c) - pb * d
            if last:
                union[c] = pick(next_left, out_r, out_l)
            else:
                union[c] = out_l
                union[4 + c] = out_r


def near_of(axis, message):
    is_left = (lax.axis_index(axis) & 1) == 0
    rows = jnp.where(is_left, message[4:8], message[0:4])
    coef = jnp.where(is_left, message[12:14], message[8:10])
    return jnp.concatenate([rows, coef], 0)


def fluxes(axis, mine, theirs, saved):
    index = lax.axis_index(axis)
    bit = lax.axis_size(axis) // 2
    is_left = (index & bit) == 0
    result = []
    for c in range(4):
        group = GROUPS[c]
        m = 1.0 / (mine[4 + group] + theirs[4 + group])
        d = theirs[c] - mine[c]
        flux = m * pick(is_left, d, -d)
        zero = jnp.zeros_like(flux)
        low = pick(is_left, zero, flux)
        high = pick(is_left, flux, zero)
        this = bit
        for part in saved[::-1]:
            this = this // 2
            flux = part[c] + part[6 + group] * high + part[4 + group] * low
            side = (index & this) == 0
            low, high = pick(side, low, flux), pick(side, flux, high)
        result.append((low, high))
    return result


def local_kernel(source, ivx, rx, cx, wx, local_t, cx_t, wx_t, scratch):
    _, nx, ny, nz = source.shape
    for c in range(4):
        group = GROUPS[c]
        running = source[c, 0]
        forward = [running]
        for i in range(1, nx):
            running = source[c, i] + rx[group, i - 1] * running
            forward.append(running)
        value = running * ivx[group, nx - 1]
        scratch[c, pl.ds((nx - 1) * ny, ny)] = value
        for i in range(nx - 2, -1, -1):
            value = forward[i] * ivx[group, i] + rx[group, i] * value
            scratch[c, pl.ds(i * ny, ny)] = value
        for j in range(ny):
            local_t[c, j] = scratch[c, pl.ds(j, nx, stride=ny), :]
    for group in range(2):
        c_rows = cx.at[group].reshape(nx * ny, nz)
        w_rows = wx.at[group].reshape(nx * ny, nz)
        for j in range(ny):
            cx_t[group, j] = c_rows[pl.ds(j, nx, stride=ny), :]
            wx_t[group, j] = w_rows[pl.ds(j, nx, stride=ny), :]


def y_start_kernel(stages, *refs):
    mine, theirs = refs[0], refs[1]
    saved = refs[2 : 2 + stages]
    visc, y_even, y_odd, local_t, cx_t, wx_t, cy, wy, solved, message, flux_low, flux_high = refs[2 + stages :]
    _, ny, nx, nz = local_t.shape
    for c, (low, high) in enumerate(fluxes("gx", mine, theirs, saved)):
        flux_low[c] = low
        flux_high[c] = high
    for c in range(4):
        group = GROUPS[c]
        left = right = None
        for j in range(ny):
            low = flux_low[c, pl.ds(j, 1)]
            high = flux_high[c, pl.ds(j, 1)]
            value = local_t[c, j] + (wx_t[group, j] * high - cx_t[group, j] * low)
            solved[c, j] = value
            a, b = cy[group, j] * value, wy[group, j] * value
            left = a if j == 0 else left + a
            right = b if j == 0 else right + b
        message[c] = left
        message[4 + c] = right
    y_par = lax.rem(lax.axis_index("gy"), 2) == 0
    beyond = pick(y_par, y_even[4], y_odd[4])
    edge = visc.reshape(nx * ny, nz)[pl.ds(ny - 1, nx, stride=ny), :]
    face = 0.5 * (edge + beyond)
    for group, scale in enumerate(SCALES):
        message[8 + group] = cy[group, 0]
        message[10 + group] = cy[group, ny - 1]
        message[12 + group] = wy[group, ny - 1] + 1.0 / (scale * face)


def y_local_kernel(solved, ivy, ry, local):
    _, ny, nx, nz = solved.shape
    for c in range(4):
        group = GROUPS[c]
        running = solved[c, 0]
        forward = [running]
        for j in range(1, ny):
            running = solved[c, j] + ry[group, j - 1] * running
            forward.append(running)
        value = running * ivy[group, ny - 1]
        local[c, ny - 1] = value
        for j in range(ny - 2, -1, -1):
            value = forward[j] * ivy[group, j] + ry[group, j] * value
            local[c, j] = value


def finish_kernel(stages, *refs):
    mine, theirs = refs[0], refs[1]
    saved = refs[2 : 2 + stages]
    local, cy, wy, out = refs[2 + stages :]
    _, ny, nx, nz = local.shape
    ends = fluxes("gy", mine, theirs, saved)
    for c in range(4):
        group = GROUPS[c]
        low, high = ends[c]
        rows = out.at[c].reshape(nx * ny, nz)
        for j in range(ny):
            value = local[c, j] + (wy[group, j] * high - cy[group, j] * low)
            rows[pl.ds(j, nx, stride=ny), :] = value


def reduce_line(axis, message):
    count = lax.axis_size(axis)
    shape = message.shape[1:]
    saved = []
    bit = 1
    if count == 2:
        message = near_of(axis, message)
    while bit * 2 < count:
        theirs = lax.ppermute(message, axis, [(i, i ^ bit) for i in range(count)])
        last = bit * 4 == count
        message, part = call(
            functools.partial(merge_kernel, axis, bit, last),
            (message, theirs),
            [(6 if last else 14,) + shape, (8,) + shape],
        )
        saved.append(part)
        bit *= 2
    theirs = lax.ppermute(message, axis, [(i, i ^ bit) for i in range(count)])
    return message, theirs, saved


def per_device(flow, visc):
    fields, nx, ny, nz = flow.shape
    mx, my = lax.axis_size("gx"), lax.axis_size("gy")
    edges = call(
        pack_kernel,
        (flow, visc),
        [(5, ny, nz), (5, ny, nz), (5, nx, nz), (5, nx, nz)],
        scratch=[pltpu.SemaphoreType.DMA((8,))],
        in_specs=[ANY, ANY],
    )
    x_even = lax.ppermute(edges[0], "gx", [(i, i ^ 1) for i in range(mx)])
    y_even = lax.ppermute(edges[2], "gy", [(i, i ^ 1) for i in range(my)])
    odd = lambda n: [(i, i + 1) for i in range(1, n - 1, 2)] + [(i + 1, i) for i in range(1, n - 1, 2)]
    x_odd = lax.ppermute(edges[1], "gx", odd(mx))
    y_odd = lax.ppermute(edges[3], "gy", odd(my))

    along_x, along_y = (2, nx, ny, nz), (2, ny, nx, nz)
    ivx, rx, cx, wx, ivy, ry, cy, wy = call(
        factor_kernel, (visc,), [along_x] * 4 + [along_y] * 4, cost=8000000
    )
    source, message = call(
        source_kernel,
        (flow, visc, x_even, x_odd, y_even, y_odd, cx, wx),
        [(fields, nx, ny, nz), (14, ny, nz)],
    )
    local_t, cx_t, wx_t = call(
        local_kernel,
        (source, ivx, rx, cx, wx),
        [(fields, ny, nx, nz), along_y, along_y],
        scratch=[pltpu.VMEM((fields, nx * ny, nz), F32)],
        cost=8000000,
    )
    mine, theirs, saved = reduce_line("gx", message)
    solved, message_y = call(
        functools.partial(y_start_kernel, len(saved)),
        (mine, theirs, *saved, visc, y_even, y_odd, local_t, cx_t, wx_t, cy, wy),
        [(fields, ny, nx, nz), (14, nx, nz)],
        scratch=[pltpu.VMEM((fields, ny, nz), F32)] * 2,
    )
    (local_y,) = call(y_local_kernel, (solved, ivy, ry), [(fields, ny, nx, nz)], cost=8000000)
    mine, theirs, saved = reduce_line("gy", message_y)
    (out,) = call(
        functools.partial(finish_kernel, len(saved)),
        (mine, theirs, *saved, local_y, cy, wy),
        [(fields, nx, ny, nz)],
    )
    return out


def solution(mesh):
    placed = (P(None, "gx", "gy", None), P("gx", "gy", None))
    return jax.shard_map(
        per_device, mesh=mesh, in_specs=placed, out_specs=P(None, "gx", "gy", None), check_vma=False
    )
```

```python
import functools

import jax
import jax.numpy as jnp
from jax import lax
from jax.experimental import pallas as pl
from jax.experimental.pallas import tpu as pltpu
from jax.sharding import PartitionSpec as P

ADVECT = 0.2
BUOYANT = 0.5
CONDUCT = 0.6
GROUPS = (0, 0, 0, 1)
SCALES = (1.0, CONDUCT)
VMEM = pl.BlockSpec(memory_space=pltpu.VMEM)
HBM = pl.BlockSpec(memory_space=pltpu.HBM)
F32 = jnp.float32


def call(kernel, ins, outs, scratch=(), in_specs=None, out_specs=None, cost=1000000):
    return pl.pallas_call(
        kernel,
        out_shape=[jax.ShapeDtypeStruct(shape, F32) for shape in outs],
        in_specs=in_specs or [VMEM] * len(ins),
        out_specs=out_specs or [VMEM] * len(outs),
        scratch_shapes=list(scratch),
        compiler_params=pltpu.CompilerParams(vmem_limit_bytes=40 * 1024 * 1024),
        cost_estimate=pl.CostEstimate(flops=cost, bytes_accessed=cost, transcendentals=0),
    )(*ins)


def pick(flag, a, b):
    return jnp.where(flag, a, b)


def pack_kernel(flow, visc, x_even, x_odd, y_even, y_odd, sems):
    nx, ny = flow.shape[1], flow.shape[2]
    x_par = lax.rem(lax.axis_index("gx"), 2)
    y_par = lax.rem(lax.axis_index("gy"), 2)
    copies = []
    for out, row in ((x_even, (1 - x_par) * (nx - 1)), (x_odd, x_par * (nx - 1))):
        copies.append((flow.at[:, row], out.at[pl.ds(0, 4)]))
        copies.append((visc.at[row], out.at[4]))
    for out, row in ((y_even, (1 - y_par) * (ny - 1)), (y_odd, y_par * (ny - 1))):
        copies.append((flow.at[:, :, row], out.at[pl.ds(0, 4)]))
        copies.append((visc.at[:, row], out.at[4]))
    started = [pltpu.make_async_copy(a, b, sems.at[i]) for i, (a, b) in enumerate(copies)]
    for copy in started:
        copy.start()
    for copy in started:
        copy.wait()


def factor_line(load, count, first, last, inv, ratio, left, right):
    for group, scale in enumerate(SCALES):
        here = load(0)
        excess = 1.0 + pick(first, scale * here, 0.0)
        column = None
        columns = []
        for i in range(count):
            if i < count - 1:
                beyond = load(i + 1)
                face = (0.5 * scale) * (here + beyond)
                inverse = 1.0 / (excess + face)
                portion = face * inverse
                ratio[group, i] = portion
                inv[group, i] = inverse
                columns.append(column)
                column = portion if column is None else column * portion
                excess = 1.0 + portion * excess
                here = beyond
            else:
                excess = excess + pick(last, scale * here, 0.0)
                inverse = 1.0 / excess
                inv[group, i] = inverse
                ratio[group, i] = inverse
                columns.append(column)
        response = inverse
        onward = column * inverse
        right[group, count - 1] = response
        left[group, count - 1] = onward
        for i in range(count - 2, -1, -1):
            portion = ratio[group, i]
            response = portion * response
            start = inv[group, i] if i == 0 else columns[i] * inv[group, i]
            onward = start + portion * onward
            right[group, i] = response
            left[group, i] = onward


def factor_kernel(visc, ivx, rx, cx, wx, ivy, ry, cy, wy):
    nx, ny, nz = visc.shape
    ix, iy = lax.axis_index("gx"), lax.axis_index("gy")
    mx, my = lax.axis_size("gx"), lax.axis_size("gy")
    factor_line(lambda i: visc[i], nx, ix == 0, ix == mx - 1, ivx, rx, cx, wx)
    rows = visc.reshape(nx * ny, nz)
    factor_line(
        lambda j: rows[pl.ds(j, nx, stride=ny), :], ny, iy == 0, iy == my - 1, ivy, ry, cy, wy
    )


def source_kernel(flow, visc, x_even, x_odd, y_even, y_odd, cx, wx, source, message):
    _, nx, ny, nz = flow.shape
    ix, iy = lax.axis_index("gx"), lax.axis_index("gy")
    x_par, y_par = lax.rem(ix, 2) == 0, lax.rem(iy, 2) == 0
    x_first, x_last = ix == 0, ix == lax.axis_size("gx") - 1
    y_first, y_last = iy == 0, iy == lax.axis_size("gy") - 1
    row = lax.broadcasted_iota(jnp.int32, (ny, nz), 0)
    left = [None] * 4
    right = [None] * 4
    for i in range(nx):
        velocity = [ADVECT * 0.5 * flow[c, i] for c in range(3)]
        temperature = None
        for c in (3, 0, 1, 2):
            f = flow[c, i]
            if i == 0:
                down = pick(x_first, 0.0, pick(x_par, x_odd[c], x_even[c]))
            else:
                down = flow[c, i - 1]
            if i == nx - 1:
                up = pick(x_last, 0.0, pick(x_par, x_even[c], x_odd[c]))
            else:
                up = flow[c, i + 1]
            y_low = pick(y_par, y_odd[c, pl.ds(i, 1)], y_even[c, pl.ds(i, 1)])
            y_high = pick(y_par, y_even[c, pl.ds(i, 1)], y_odd[c, pl.ds(i, 1)])
            y_low = pick(y_first, 0.0, y_low)
            y_high = pick(y_last, 0.0, y_high)
            below = pick(row == 0, y_low, pltpu.roll(f, 1, 0))
            above = pick(row == ny - 1, y_high, pltpu.roll(f, ny - 1, 0))
            z_low = pltpu.roll(f, 1, 1)
            z_high = pltpu.roll(f, nz - 1, 1)
            s = f - (
                velocity[0] * (up - down)
                + velocity[1] * (above - below)
                + velocity[2] * (z_high - z_low)
            )
            if c == 3:
                temperature = f
            if c == 2:
                s = s + BUOYANT * temperature
            source[c, i] = s
            group = GROUPS[c]
            a, b = cx[group, i] * s, wx[group, i] * s
            left[c] = a if i == 0 else left[c] + a
            right[c] = b if i == 0 else right[c] + b
    for c in range(4):
        message[c] = left[c]
        message[4 + c] = right[c]
    beyond = pick(x_par, x_even[4], x_odd[4])
    face = 0.5 * (visc[nx - 1] + beyond)
    for group, scale in enumerate(SCALES):
        message[8 + group] = cx[group, 0]
        message[10 + group] = cx[group, nx - 1]
        message[12 + group] = wx[group, nx - 1] + 1.0 / (scale * face)


def merge_kernel(axis, bit, last, mine, theirs, union, saved):
    is_left = (lax.axis_index(axis) & bit) == 0
    next_left = (lax.axis_index(axis) & (2 * bit)) == 0

    def a(k):
        return pick(is_left, mine[k], theirs[k])

    def b(k):
        return pick(is_left, theirs[k], mine[k])

    for group in range(2):
        a_lr, b_lr = a(10 + group), b(10 + group)
        m = 1.0 / (a(12 + group) + b(8 + group))
        pa, pb = m * a_lr, m * b_lr
        saved[4 + group] = pa
        saved[6 + group] = pb
        out_ll = a(8 + group) - a_lr * pa
        out_rr = b(12 + group) - b_lr * pb
        if last:
            union[4 + group] = pick(next_left, out_rr, out_ll)
        else:
            union[8 + group] = out_ll
            union[10 + group] = a_lr * pb
            union[12 + group] = out_rr
        for c in range(4):
            if GROUPS[c] != group:
                continue
            d = b(c) - a(4 + c)
            saved[c] = m * d
            out_l = a(c) + pa * d
            out_r = b(4 + c) - pb * d
            if last:
                union[c] = pick(next_left, out_r, out_l)
            else:
                union[c] = out_l
                union[4 + c] = out_r


def near_of(axis, message):
    is_left = (lax.axis_index(axis) & 1) == 0
    rows = jnp.where(is_left, message[4:8], message[0:4])
    coef = jnp.where(is_left, message[12:14], message[8:10])
    return jnp.concatenate([rows, coef], 0)


def fluxes(axis, mine, theirs, saved):
    index = lax.axis_index(axis)
    bit = lax.axis_size(axis) // 2
    is_left = (index & bit) == 0
    result = []
    for c in range(4):
        group = GROUPS[c]
        m = 1.0 / (mine[4 + group] + theirs[4 + group])
        d = theirs[c] - mine[c]
        flux = m * pick(is_left, d, -d)
        zero = jnp.zeros_like(flux)
        low = pick(is_left, zero, flux)
        high = pick(is_left, flux, zero)
        this = bit
        for part in saved[::-1]:
            this = this // 2
            flux = part[c] + part[6 + group] * high + part[4 + group] * low
            side = (index & this) == 0
            low, high = pick(side, low, flux), pick(side, flux, high)
        result.append((low, high))
    return result


def local_kernel(source, ivx, rx, cx, wx, local_t, cx_t, wx_t, scratch):
    _, nx, ny, nz = source.shape
    for c in range(4):
        group = GROUPS[c]
        running = source[c, 0]
        forward = [running]
        for i in range(1, nx):
            running = source[c, i] + rx[group, i - 1] * running
            forward.append(running)
        value = running * ivx[group, nx - 1]
        scratch[c, pl.ds((nx - 1) * ny, ny)] = value
        for i in range(nx - 2, -1, -1):
            value = forward[i] * ivx[group, i] + rx[group, i] * value
            scratch[c, pl.ds(i * ny, ny)] = value
        for j in range(ny):
            local_t[c, j] = scratch[c, pl.ds(j, nx, stride=ny), :]
    for group in range(2):
        c_rows = cx.at[group].reshape(nx * ny, nz)
        w_rows = wx.at[group].reshape(nx * ny, nz)
        for j in range(ny):
            cx_t[group, j] = c_rows[pl.ds(j, nx, stride=ny), :]
            wx_t[group, j] = w_rows[pl.ds(j, nx, stride=ny), :]


def y_start_kernel(stages, *refs):
    mine, theirs = refs[0], refs[1]
    saved = refs[2 : 2 + stages]
    visc, y_even, y_odd, local_t, cx_t, wx_t, cy, wy, solved, message, flux_low, flux_high = refs[2 + stages :]
    _, ny, nx, nz = local_t.shape
    for c, (low, high) in enumerate(fluxes("gx", mine, theirs, saved)):
        flux_low[c] = low
        flux_high[c] = high
    for c in range(4):
        group = GROUPS[c]
        left = right = None
        for j in range(ny):
            low = flux_low[c, pl.ds(j, 1)]
            high = flux_high[c, pl.ds(j, 1)]
            value = local_t[c, j] + (wx_t[group, j] * high - cx_t[group, j] * low)
            solved[c, j] = value
            a, b = cy[group, j] * value, wy[group, j] * value
            left = a if j == 0 else left + a
            right = b if j == 0 else right + b
        message[c] = left
        message[4 + c] = right
    y_par = lax.rem(lax.axis_index("gy"), 2) == 0
    beyond = pick(y_par, y_even[4], y_odd[4])
    edge = visc.reshape(nx * ny, nz)[pl.ds(ny - 1, nx, stride=ny), :]
    face = 0.5 * (edge + beyond)
    for group, scale in enumerate(SCALES):
        message[8 + group] = cy[group, 0]
        message[10 + group] = cy[group, ny - 1]
        message[12 + group] = wy[group, ny - 1] + 1.0 / (scale * face)


def y_local_kernel(solved, ivy, ry, local):
    _, ny, nx, nz = solved.shape
    for c in range(4):
        group = GROUPS[c]
        running = solved[c, 0]
        forward = [running]
        for j in range(1, ny):
            running = solved[c, j] + ry[group, j - 1] * running
            forward.append(running)
        value = running * ivy[group, ny - 1]
        local[c, ny - 1] = value
        for j in range(ny - 2, -1, -1):
            value = forward[j] * ivy[group, j] + ry[group, j] * value
            local[c, j] = value


def finish_kernel(stages, *refs):
    mine, theirs = refs[0], refs[1]
    saved = refs[2 : 2 + stages]
    local, cy, wy, out, buffer, sems = refs[2 + stages :]
    _, ny, nx, nz = local.shape
    ends = fluxes("gy", mine, theirs, saved)
    copies = []
    for c in range(4):
        group = GROUPS[c]
        low, high = ends[c]
        rows = buffer.at[c].reshape(nx * ny, nz)
        for j in range(ny):
            value = local[c, j] + (wy[group, j] * high - cy[group, j] * low)
            rows[pl.ds(j, nx, stride=ny), :] = value
        copies.append(pltpu.make_async_copy(buffer.at[c], out.at[c], sems.at[c]))
        copies[-1].start()
    for copy in copies:
        copy.wait()


def reduce_line(axis, message):
    count = lax.axis_size(axis)
    shape = message.shape[1:]
    saved = []
    bit = 1
    if count == 2:
        message = near_of(axis, message)
    while bit * 2 < count:
        theirs = lax.ppermute(message, axis, [(i, i ^ bit) for i in range(count)])
        last = bit * 4 == count
        message, part = call(
            functools.partial(merge_kernel, axis, bit, last),
            (message, theirs),
            [(6 if last else 14,) + shape, (8,) + shape],
        )
        saved.append(part)
        bit *= 2
    theirs = lax.ppermute(message, axis, [(i, i ^ bit) for i in range(count)])
    return message, theirs, saved


def per_device(flow, visc):
    fields, nx, ny, nz = flow.shape
    mx, my = lax.axis_size("gx"), lax.axis_size("gy")
    edges = call(
        pack_kernel,
        (flow, visc),
        [(5, ny, nz), (5, ny, nz), (5, nx, nz), (5, nx, nz)],
        scratch=[pltpu.SemaphoreType.DMA((8,))],
        in_specs=[HBM, HBM],
    )
    pairs = []
    for i in range(mx):
        for j in range(my):
            inner = 0 < i < mx - 1
            partner = ((i - 1 ^ 1) + 1, j) if inner else (i, j ^ 1)
            pairs.append((i * my + j, partner[0] * my + partner[1]))
    x_odd = lax.ppermute(edges[1], ("gx", "gy"), pairs)
    y_odd = lax.ppermute(edges[3], "gy", [(i, (i - 1 ^ 1) + 1) if 0 < i < my - 1 else (i, my - 1 - i) for i in range(my)])
    x_even = lax.ppermute(edges[0], "gx", [(i, i ^ 1) for i in range(mx)])
    y_even = lax.ppermute(edges[2], "gy", [(i, i ^ 1) for i in range(my)])

    along_x, along_y = (2, nx, ny, nz), (2, ny, nx, nz)
    ivx, rx, cx, wx, ivy, ry, cy, wy = call(
        factor_kernel, (visc,), [along_x] * 4 + [along_y] * 4, cost=8000000
    )
    source, message = call(
        source_kernel,
        (flow, visc, x_even, x_odd, y_even, y_odd, cx, wx),
        [(fields, nx, ny, nz), (14, ny, nz)],
    )
    local_t, cx_t, wx_t = call(
        local_kernel,
        (source, ivx, rx, cx, wx),
        [(fields, ny, nx, nz), along_y, along_y],
        scratch=[pltpu.VMEM((fields, nx * ny, nz), F32)],
        cost=8000000,
    )
    mine, theirs, saved = reduce_line("gx", message)
    solved, message_y = call(
        functools.partial(y_start_kernel, len(saved)),
        (mine, theirs, *saved, visc, y_even, y_odd, local_t, cx_t, wx_t, cy, wy),
        [(fields, ny, nx, nz), (14, nx, nz)],
        scratch=[pltpu.VMEM((fields, ny, nz), F32)] * 2,
    )
    (local_y,) = call(y_local_kernel, (solved, ivy, ry), [(fields, ny, nx, nz)], cost=8000000)
    mine, theirs, saved = reduce_line("gy", message_y)
    (out,) = call(
        functools.partial(finish_kernel, len(saved)),
        (mine, theirs, *saved, local_y, cy, wy),
        [(fields, nx, ny, nz)],
        scratch=[pltpu.VMEM((fields, nx, ny, nz), F32), pltpu.SemaphoreType.DMA((fields,))],
        out_specs=[HBM],
    )
    return out


def solution(mesh):
    placed = (P(None, "gx", "gy", None), P("gx", "gy", None))
    return jax.shard_map(
        per_device, mesh=mesh, in_specs=placed, out_specs=P(None, "gx", "gy", None), check_vma=False
    )
```

```python
import functools

import jax
import jax.numpy as jnp
from jax import lax
from jax.experimental import pallas as pl
from jax.experimental.pallas import tpu as pltpu
from jax.sharding import PartitionSpec as P

ADVECT = 0.2
BUOYANT = 0.5
CONDUCT = 0.6
GROUPS = (0, 0, 0, 1)
SCALES = (1.0, CONDUCT)
VMEM = pl.BlockSpec(memory_space=pltpu.VMEM)
HBM = pl.BlockSpec(memory_space=pltpu.HBM)
F32 = jnp.float32


def call(kernel, ins, outs, scratch=(), in_specs=None, out_specs=None, cost=1000, vmem=40):
    return pl.pallas_call(
        kernel,
        out_shape=[jax.ShapeDtypeStruct(shape, F32) for shape in outs],
        in_specs=in_specs or [VMEM] * len(ins),
        out_specs=out_specs or [VMEM] * len(outs),
        scratch_shapes=list(scratch),
        compiler_params=pltpu.CompilerParams(vmem_limit_bytes=vmem * 1024 * 1024),
        cost_estimate=pl.CostEstimate(flops=cost, bytes_accessed=cost, transcendentals=0),
    )(*ins)


def pick(flag, a, b):
    return jnp.where(flag, a, b)


def factor_line(load, count, first, last, inv, ratio, left, right):
    for group, scale in enumerate(SCALES):
        here = load(0)
        excess = 1.0 + pick(first, scale * here, 0.0)
        column = None
        columns = []
        for i in range(count):
            if i < count - 1:
                beyond = load(i + 1)
                face = (0.5 * scale) * (here + beyond)
                inverse = 1.0 / (excess + face)
                portion = face * inverse
                ratio[group, i] = portion
                inv[group, i] = inverse
                columns.append(column)
                column = portion if column is None else column * portion
                excess = 1.0 + portion * excess
                here = beyond
            else:
                excess = excess + pick(last, scale * here, 0.0)
                inverse = 1.0 / excess
                inv[group, i] = inverse
                ratio[group, i] = inverse
                columns.append(column)
        response = inverse
        onward = column * inverse
        right[group, count - 1] = response
        left[group, count - 1] = onward
        for i in range(count - 2, -1, -1):
            portion = ratio[group, i]
            response = portion * response
            start = inv[group, i] if i == 0 else columns[i] * inv[group, i]
            onward = start + portion * onward
            right[group, i] = response
            left[group, i] = onward


def coef_rows(left, right, out, count):
    for group in range(2):
        out[group] = left[group, 0]
        out[2 + group] = left[group, count - 1]
        out[4 + group] = right[group, count - 1]


def first_kernel(flow, visc, x_odd, y_even, y_odd, ivx, rx, cx, wx, coef_x, cells, sems):
    nx, ny = flow.shape[1], flow.shape[2]
    ix, iy = lax.axis_index("gx"), lax.axis_index("gy")
    x_par, y_par = lax.rem(ix, 2), lax.rem(iy, 2)
    copies = (
        (visc, cells),
        (flow.at[:, x_par * (nx - 1)], x_odd),
        (flow.at[:, :, (1 - y_par) * (ny - 1)], y_even),
        (flow.at[:, :, y_par * (ny - 1)], y_odd),
    )
    started = [pltpu.make_async_copy(a, b, sems.at[i]) for i, (a, b) in enumerate(copies)]
    for copy in started:
        copy.start()
    started[0].wait()
    factor_line(lambda i: cells[i], nx, ix == 0, ix == lax.axis_size("gx") - 1, ivx, rx, cx, wx)
    coef_rows(cx, wx, coef_x, nx)
    coef_x[6] = cells[0]
    coef_x[7] = cells[nx - 1]
    for copy in started[1:]:
        copy.wait()


def factor_y_kernel(visc, ivy, ry, cy, wy, coef_y):
    nx, ny, nz = visc.shape
    iy = lax.axis_index("gy")
    rows = visc.reshape(nx * ny, nz)

    def row_y(j):
        return rows[pl.ds(j, nx, stride=ny), :]

    factor_line(row_y, ny, iy == 0, iy == lax.axis_size("gy") - 1, ivy, ry, cy, wy)
    coef_rows(cy, wy, coef_y, ny)
    coef_y[6] = row_y(0)
    coef_y[7] = row_y(ny - 1)


def source_kernel(flow, x_odd, y_even, y_odd, cx, wx, after, source, message):
    _, nx, ny, nz = flow.shape
    ix, iy = lax.axis_index("gx"), lax.axis_index("gy")
    x_par, y_par = lax.rem(ix, 2) == 0, lax.rem(iy, 2) == 0
    no_low = (ix == 0) | (lax.rem(ix, 2) == 1)
    no_high = (ix == lax.axis_size("gx") - 1) | x_par
    y_first, y_last = iy == 0, iy == lax.axis_size("gy") - 1
    row = lax.broadcasted_iota(jnp.int32, (ny, nz), 0)
    left = [None] * 4
    right = [None] * 4
    for i in range(nx):
        velocity = [ADVECT * 0.5 * flow[c, i] for c in range(3)]
        for c in range(4):
            f = flow[c, i]
            down = pick(no_low, 0.0, x_odd[c]) if i == 0 else flow[c, i - 1]
            up = pick(no_high, 0.0, x_odd[c]) if i == nx - 1 else flow[c, i + 1]
            y_low = pick(y_par, y_odd[c, pl.ds(i, 1)], y_even[c, pl.ds(i, 1)])
            y_high = pick(y_par, y_even[c, pl.ds(i, 1)], y_odd[c, pl.ds(i, 1)])
            y_low = pick(y_first, 0.0, y_low)
            y_high = pick(y_last, 0.0, y_high)
            below = pick(row == 0, y_low, pltpu.roll(f, 1, 0))
            above = pick(row == ny - 1, y_high, pltpu.roll(f, ny - 1, 0))
            z_low = pltpu.roll(f, 1, 1)
            z_high = pltpu.roll(f, nz - 1, 1)
            s = f - (
                velocity[0] * (up - down)
                + velocity[1] * (above - below)
                + velocity[2] * (z_high - z_low)
            )
            if c == 2:
                s = s + BUOYANT * flow[3, i]
            source[c, i] = s
            group = GROUPS[c]
            a, b = cx[group, i] * s, wx[group, i] * s
            left[c] = a if i == 0 else left[c] + a
            right[c] = b if i == 0 else right[c] + b
    for c in range(4):
        message[c] = left[c]
        message[4 + c] = right[c]
        message[8 + c] = pick(x_par, flow[c, nx - 1], flow[c, 0])


def coef_part(axis, bit, last, mine, theirs, at, union, union_at, weights):
    is_left = (lax.axis_index(axis) & bit) == 0
    next_left = (lax.axis_index(axis) & (2 * bit)) == 0

    def a(k):
        return pick(is_left, mine[at + k], theirs[at + k])

    def b(k):
        return pick(is_left, theirs[at + k], mine[at + k])

    face = 0.5 * (a(7) + b(6))
    for group, scale in enumerate(SCALES):
        a_lr, b_lr = a(2 + group), b(2 + group)
        m = 1.0 / (1.0 / (scale * face) + a(4 + group) + b(group))
        pa, pb = m * a_lr, m * b_lr
        weights[group] = m
        weights[2 + group] = pa
        weights[4 + group] = pb
        out_ll = a(group) - a_lr * pa
        out_rr = b(4 + group) - b_lr * pb
        if last:
            union[union_at + group] = pick(next_left, out_rr, out_ll)
        else:
            union[union_at + group] = out_ll
            union[union_at + 2 + group] = a_lr * pb
            union[union_at + 4 + group] = out_rr
    if last:
        union[union_at + 2] = pick(next_left, b(7), a(6))
    else:
        union[union_at + 6] = a(6)
        union[union_at + 7] = b(7)


def row_part(axis, bit, last, mine, theirs, weights, union, saved, edged=None):
    is_left = (lax.axis_index(axis) & bit) == 0
    next_left = (lax.axis_index(axis) & (2 * bit)) == 0

    def sides(x, y):
        return pick(is_left, x, y), pick(is_left, y, x)

    for c in range(4):
        group = GROUPS[c]
        a_l, b_l = sides(mine[c], theirs[c])
        a_r, b_r = sides(mine[4 + c], theirs[4 + c])
        if edged is not None:
            coef_mine, coef_theirs, missing = edged
            here = (ADVECT * 0.5) * mine[8] * theirs[8 + c]
            there = (ADVECT * 0.5) * theirs[8] * mine[8 + c]
            missing[c] = here
            a_gap, b_gap = sides(here, there)
            ll = pick(is_left, coef_theirs[group], coef_mine[group])
            rr = pick(is_left, coef_mine[4 + group], coef_theirs[4 + group])
            a_lr, b_lr = sides(coef_mine[2 + group], coef_theirs[2 + group])
            a_l = a_l - a_lr * a_gap
            a_r = a_r - rr * a_gap
            b_l = b_l + ll * b_gap
            b_r = b_r + b_lr * b_gap
        d = b_l - a_r
        saved[c] = weights[group] * d
        out_l = a_l + weights[2 + group] * d
        out_r = b_r - weights[4 + group] * d
        if last:
            union[c] = pick(next_left, out_r, out_l)
        else:
            union[c] = out_l
            union[4 + c] = out_r


def coef_kernel(axis, bit, last, mine, theirs, after, union, weights):
    coef_part(axis, bit, last, mine, theirs, 0, union, 0, weights)


def x_merge_kernel(axis, bit, last, edged, mine, theirs, weights, coef_mine, coef_theirs, near, union, saved, missing):
    row_part(
        axis, bit, last, mine, theirs, weights, union, saved,
        (coef_mine, coef_theirs, missing) if edged else None,
    )
    if last:
        union[pl.ds(4, 3)] = near[...]


def y_merge_kernel(axis, bit, last, mine, theirs, union, saved, weights):
    coef_part(axis, bit, last, mine, theirs, 8, union, 4 if last else 8, weights)
    row_part(axis, bit, last, mine, theirs, weights, union, saved)


def fluxes(axis, mine, theirs, saved, missing=None):
    index = lax.axis_index(axis)
    bit = lax.axis_size(axis) // 2
    is_left = (index & bit) == 0
    result = []
    face = 0.5 * (mine[6] + theirs[6])
    weight = [
        1.0 / (1.0 / (scale * face) + mine[4 + group] + theirs[4 + group])
        for group, scale in enumerate(SCALES)
    ]
    for c in range(4):
        group = GROUPS[c]
        d = theirs[c] - mine[c]
        flux = weight[group] * pick(is_left, d, -d)
        zero = jnp.zeros_like(flux)
        low = pick(is_left, zero, flux)
        high = pick(is_left, flux, zero)
        this = bit
        for part, weights in saved[::-1]:
            this = this // 2
            flux = part[c] + weights[4 + group] * high + weights[2 + group] * low
            if this == 1 and missing is not None:
                flux = flux - missing[c]
            side = (index & this) == 0
            low, high = pick(side, low, flux), pick(side, flux, high)
        result.append((low, high))
    return result


def local_kernel(source, ivx, rx, cx, wx, local_t, cx_t, wx_t, scratch):
    _, nx, ny, nz = source.shape
    for c in range(4):
        group = GROUPS[c]
        running = source[c, 0]
        forward = [running]
        for i in range(1, nx):
            running = source[c, i] + rx[group, i - 1] * running
            forward.append(running)
        value = running * ivx[group, nx - 1]
        scratch[c, pl.ds((nx - 1) * ny, ny)] = value
        for i in range(nx - 2, -1, -1):
            value = forward[i] * ivx[group, i] + rx[group, i] * value
            scratch[c, pl.ds(i * ny, ny)] = value
        for j in range(ny):
            local_t[c, j] = scratch[c, pl.ds(j, nx, stride=ny), :]
    for group in range(2):
        c_rows = cx.at[group].reshape(nx * ny, nz)
        w_rows = wx.at[group].reshape(nx * ny, nz)
        for j in range(ny):
            cx_t[group, j] = c_rows[pl.ds(j, nx, stride=ny), :]
            wx_t[group, j] = w_rows[pl.ds(j, nx, stride=ny), :]


def y_start_kernel(stages, *refs):
    mine, theirs, missing = refs[:3]
    parts = refs[3 : 3 + 2 * stages]
    local_t, cx_t, wx_t, cy, wy, coef_y, solved, message, flux_low, flux_high = refs[3 + 2 * stages :]
    _, ny, nx, nz = local_t.shape
    saved = list(zip(parts[::2], parts[1::2]))
    for c, (low, high) in enumerate(fluxes("gx", mine, theirs, saved, missing)):
        flux_low[c] = low
        flux_high[c] = high
    for c in range(4):
        group = GROUPS[c]
        left = right = None
        for j in range(ny):
            low = flux_low[c, pl.ds(j, 1)]
            high = flux_high[c, pl.ds(j, 1)]
            value = local_t[c, j] + (wx_t[group, j] * high - cx_t[group, j] * low)
            solved[c, j] = value
            a, b = cy[group, j] * value, wy[group, j] * value
            left = a if j == 0 else left + a
            right = b if j == 0 else right + b
        message[c] = left
        message[4 + c] = right
    message[pl.ds(8, 8)] = coef_y[...]


def y_local_kernel(solved, ivy, ry, local):
    _, ny, nx, nz = solved.shape
    for c in range(4):
        group = GROUPS[c]
        running = solved[c, 0]
        forward = [running]
        for j in range(1, ny):
            running = solved[c, j] + ry[group, j - 1] * running
            forward.append(running)
        value = running * ivy[group, ny - 1]
        local[c, ny - 1] = value
        for j in range(ny - 2, -1, -1):
            value = forward[j] * ivy[group, j] + ry[group, j] * value
            local[c, j] = value


def finish_kernel(stages, *refs):
    mine, theirs = refs[:2]
    parts = refs[2 : 2 + 2 * stages]
    local, cy, wy, out, buffer, sems = refs[2 + 2 * stages :]
    saved = list(zip(parts[::2], parts[1::2]))
    _, ny, nx, nz = local.shape
    ends = fluxes("gy", mine, theirs, saved)
    copies = []
    for c in range(4):
        group = GROUPS[c]
        low, high = ends[c]
        rows = buffer.at[c].reshape(nx * ny, nz)
        for j in range(ny):
            value = local[c, j] + (wy[group, j] * high - cy[group, j] * low)
            rows[pl.ds(j, nx, stride=ny), :] = value
        copies.append(pltpu.make_async_copy(buffer.at[c], out.at[c], sems.at[c]))
        copies[-1].start()
    for copy in copies:
        copy.wait()


def swap(array, axis, bit):
    return lax.ppermute(array, axis, [(i, i ^ bit) for i in range(lax.axis_size(axis))])


def after_all(spec_count):
    return [VMEM] * spec_count + [pl.BlockSpec(memory_space=pl.ANY)]


def per_device(flow, visc):
    fields, nx, ny, nz = flow.shape
    mx, my = lax.axis_size("gx"), lax.axis_size("gy")
    along_x, along_y = (2, nx, ny, nz), (2, ny, nx, nz)
    x_edge, y_edge_even, y_edge_odd, ivx, rx, cx, wx, coef_x = call(
        first_kernel,
        tuple(pltpu.with_memory_space_constraint(array, pltpu.HBM) for array in (flow, visc)),
        [(fields, ny, nz), (fields, nx, nz), (fields, nx, nz)] + [along_x] * 4 + [(8, ny, nz)],
        scratch=[pltpu.VMEM((nx, ny, nz), F32), pltpu.SemaphoreType.DMA((4,))],
        in_specs=[HBM, HBM],
    )
    pairs = []
    for i in range(mx):
        for j in range(my):
            inner = 0 < i < mx - 1
            partner = ((i - 1 ^ 1) + 1, j) if inner else (i, j ^ 1)
            pairs.append((i * my + j, partner[0] * my + partner[1]))
    x_odd = lax.ppermute(x_edge, ("gx", "gy"), pairs)
    y_odd = lax.ppermute(
        y_edge_odd, "gy", [(i, (i - 1 ^ 1) + 1) if 0 < i < my - 1 else (i, my - 1 - i) for i in range(my)]
    )
    y_even = swap(y_edge_even, "gy", 1)

    ivy, ry, cy, wy, coef_y = call(factor_y_kernel, (visc,), [along_y] * 4 + [(8, nx, nz)])
    coef_x_theirs = swap(coef_x, "gx", 1)
    source, message = call(
        source_kernel,
        (flow, x_odd, y_even, y_odd, cx, wx, coef_x_theirs),
        in_specs=after_all(6),
        outs=[(fields, nx, ny, nz), (12, ny, nz)],
    )
    local_t, cx_t, wx_t = call(
        local_kernel,
        (source, ivx, rx, cx, wx),
        [(fields, ny, nx, nz), along_y, along_y],
        scratch=[pltpu.VMEM((fields, nx * ny, nz), F32)],
        cost=1000,
    )

    saved = []
    coefs, coefs_theirs, rows = coef_x, coef_x_theirs, message
    shape = (ny, nz)
    bit = 1
    while 2 * bit < mx:
        last = 4 * bit == mx
        rows_theirs = swap(rows, "gx", bit)
        merged, weights = call(
            functools.partial(coef_kernel, "gx", bit, last),
            (coefs, coefs_theirs, rows),
            [(3 if last else 8,) + shape, (6,) + shape],
            in_specs=after_all(2),
        )
        merged_theirs = merged if last else swap(merged, "gx", 2 * bit)
        rows, part, gap = call(
            functools.partial(x_merge_kernel, "gx", bit, last, bit == 1),
            (rows, rows_theirs, weights, coefs, coefs_theirs, merged),
            [(7 if last else 8,) + shape, (4,) + shape, (4,) + shape],
        )
        if bit == 1:
            missing = gap
        saved += [part, weights]
        coefs, coefs_theirs = merged, merged_theirs
        bit *= 2
    rows_theirs = swap(rows, "gx", bit)

    solved, rows = call(
        functools.partial(y_start_kernel, len(saved) // 2),
        (rows, rows_theirs, missing, *saved, local_t, cx_t, wx_t, cy, wy, coef_y),
        [(fields, ny, nx, nz), (16, nx, nz)],
        scratch=[pltpu.VMEM((fields, ny, nz), F32)] * 2,
    )
    (local_y,) = call(y_local_kernel, (solved, ivy, ry), [(fields, ny, nx, nz)])
    saved = []
    shape = (nx, nz)
    bit = 1
    while 2 * bit < my:
        last = 4 * bit == my
        rows, part, weights = call(
            functools.partial(y_merge_kernel, "gy", bit, last),
            (rows, swap(rows, "gy", bit)),
            [(7 if last else 16,) + shape, (4,) + shape, (6,) + shape],
        )
        saved += [part, weights]
        bit *= 2
    rows_theirs = swap(rows, "gy", bit)
    (out,) = call(
        functools.partial(finish_kernel, len(saved) // 2),
        (rows, rows_theirs, *saved, local_y, cy, wy),
        [(fields, nx, ny, nz)],
        scratch=[pltpu.VMEM((fields, nx, ny, nz), F32), pltpu.SemaphoreType.DMA((fields,))],
        out_specs=[HBM],
    )
    return out


def solution(mesh):
    placed = (P(None, "gx", "gy", None), P("gx", "gy", None))
    return jax.shard_map(
        per_device, mesh=mesh, in_specs=placed, out_specs=P(None, "gx", "gy", None), check_vma=False
    )
```

```python
import functools

import jax
import jax.numpy as jnp
from jax import lax
from jax.experimental import pallas as pl
from jax.experimental.pallas import tpu as pltpu
from jax.sharding import PartitionSpec as P

ADVECT = 0.2
BUOYANT = 0.5
CONDUCT = 0.6
GROUPS = (0, 0, 0, 1)
SCALES = (1.0, CONDUCT)
VMEM = pl.BlockSpec(memory_space=pltpu.VMEM)
HBM = pl.BlockSpec(memory_space=pltpu.HBM)
F32 = jnp.float32


def call(kernel, ins, outs, scratch=(), in_specs=None, out_specs=None, cost=1000, vmem=40):
    return pl.pallas_call(
        kernel,
        out_shape=[jax.ShapeDtypeStruct(shape, F32) for shape in outs],
        in_specs=in_specs or [VMEM] * len(ins),
        out_specs=out_specs or [VMEM] * len(outs),
        scratch_shapes=list(scratch),
        compiler_params=pltpu.CompilerParams(vmem_limit_bytes=vmem * 1024 * 1024),
        cost_estimate=pl.CostEstimate(flops=cost, bytes_accessed=cost, transcendentals=0),
    )(*ins)


def pick(flag, a, b):
    return jnp.where(flag, a, b)


def factor_line(load, count, first, last, inv, ratio, left, right):
    for group, scale in enumerate(SCALES):
        here = load(0)
        excess = 1.0 + pick(first, scale * here, 0.0)
        column = None
        columns = []
        for i in range(count):
            if i < count - 1:
                beyond = load(i + 1)
                face = (0.5 * scale) * (here + beyond)
                inverse = 1.0 / (excess + face)
                portion = face * inverse
                ratio[group, i] = portion
                inv[group, i] = inverse
                columns.append(column)
                column = portion if column is None else column * portion
                excess = 1.0 + portion * excess
                here = beyond
            else:
                excess = excess + pick(last, scale * here, 0.0)
                inverse = 1.0 / excess
                inv[group, i] = inverse
                ratio[group, i] = inverse
                columns.append(column)
        response = inverse
        onward = column * inverse
        right[group, count - 1] = response
        left[group, count - 1] = onward
        for i in range(count - 2, -1, -1):
            portion = ratio[group, i]
            response = portion * response
            start = inv[group, i] if i == 0 else columns[i] * inv[group, i]
            onward = start + portion * onward
            right[group, i] = response
            left[group, i] = onward


def coef_rows(left, right, out, count):
    for group in range(2):
        out[group] = left[group, 0]
        out[2 + group] = left[group, count - 1]
        out[4 + group] = right[group, count - 1]


def first_kernel(flow, visc, x_odd, y_even, y_odd, ivx, rx, cx, wx, coef_x, cells, sems):
    nx, ny = flow.shape[1], flow.shape[2]
    ix, iy = lax.axis_index("gx"), lax.axis_index("gy")
    x_par, y_par = lax.rem(ix, 2), lax.rem(iy, 2)
    copies = (
        (visc, cells),
        (flow.at[:, x_par * (nx - 1)], x_odd),
        (flow.at[:, :, (1 - y_par) * (ny - 1)], y_even),
        (flow.at[:, :, y_par * (ny - 1)], y_odd),
    )
    started = [pltpu.make_async_copy(a, b, sems.at[i]) for i, (a, b) in enumerate(copies)]
    for copy in started:
        copy.start()
    started[0].wait()
    factor_line(lambda i: cells[i], nx, ix == 0, ix == lax.axis_size("gx") - 1, ivx, rx, cx, wx)
    coef_rows(cx, wx, coef_x, nx)
    coef_x[6] = cells[0]
    coef_x[7] = cells[nx - 1]
    for copy in started[1:]:
        copy.wait()


def factor_y_kernel(visc, ivy, ry, cy, wy, coef_y, cy_t, wy_t):
    nx, ny, nz = visc.shape
    iy = lax.axis_index("gy")
    rows = visc.reshape(nx * ny, nz)

    def row_y(j):
        return rows[pl.ds(j, nx, stride=ny), :]

    factor_line(row_y, ny, iy == 0, iy == lax.axis_size("gy") - 1, ivy, ry, cy, wy)
    coef_rows(cy, wy, coef_y, ny)
    coef_y[6] = row_y(0)
    coef_y[7] = row_y(ny - 1)
    for part, turned in ((cy, cy_t), (wy, wy_t)):
        for group in range(2):
            out = turned.at[group].reshape(nx * ny, nz)
            for j in range(ny):
                out[pl.ds(j, nx, stride=ny), :] = part[group, j]


def source_kernel(flow, cx, wx, source, message):
    _, nx, ny, nz = flow.shape
    x_par = lax.rem(lax.axis_index("gx"), 2) == 0
    row = lax.broadcasted_iota(jnp.int32, (ny, nz), 0)
    left = [None] * 4
    right = [None] * 4
    for i in range(nx):
        velocity = [ADVECT * 0.5 * flow[c, i] for c in range(3)]
        for c in range(4):
            f = flow[c, i]
            down = 0.0 if i == 0 else flow[c, i - 1]
            up = 0.0 if i == nx - 1 else flow[c, i + 1]
            below = pick(row == 0, 0.0, pltpu.roll(f, 1, 0))
            above = pick(row == ny - 1, 0.0, pltpu.roll(f, ny - 1, 0))
            z_low = pltpu.roll(f, 1, 1)
            z_high = pltpu.roll(f, nz - 1, 1)
            s = f - (
                velocity[0] * (up - down)
                + velocity[1] * (above - below)
                + velocity[2] * (z_high - z_low)
            )
            if c == 2:
                s = s + BUOYANT * flow[3, i]
            source[c, i] = s
            group = GROUPS[c]
            a, b = cx[group, i] * s, wx[group, i] * s
            left[c] = a if i == 0 else left[c] + a
            right[c] = b if i == 0 else right[c] + b
    for c in range(4):
        message[c] = left[c]
        message[4 + c] = right[c]
        message[8 + c] = pick(x_par, flow[c, nx - 1], flow[c, 0])


def edge_kernel(partial, x_edge, y_edge_even, y_edge_odd, x_odd, y_even, y_odd, cx, wx, after, message, gap_x, gap_y):
    _, nx, ny, nz = cx.shape
    ix, iy = lax.axis_index("gx"), lax.axis_index("gy")
    x_par, y_par = lax.rem(ix, 2) == 0, lax.rem(iy, 2) == 0
    x_none = (ix == 0) | (ix == lax.axis_size("gx") - 1)
    y_first, y_last = iy == 0, iy == lax.axis_size("gy") - 1
    half = 0.5 * ADVECT
    message[pl.ds(8, 4)] = partial[pl.ds(8, 4)]
    own_low = half * pick(y_par, y_edge_odd[1], y_edge_even[1])
    own_high = half * pick(y_par, y_edge_even[1], y_edge_odd[1])
    own_x = half * x_edge[0]
    for c in range(4):
        group = GROUPS[c]
        low = own_low * pick(y_par, y_odd[c], y_even[c])
        high = -own_high * pick(y_par, y_even[c], y_odd[c])
        low = pick(y_first, 0.0, low)
        high = pick(y_last, 0.0, high)
        gap_y[c] = low
        gap_y[4 + c] = high
        across = own_x * x_odd[c]
        across = pick(x_none, 0.0, pick(x_par, across, -across))
        gap_x[c] = across
        for k, part in ((c, cx), (4 + c, wx)):
            edge = pick(x_par, part[group, 0], part[group, nx - 1])
            message[k] = partial[k] + edge * across
            rows = part.at[group].reshape(nx * ny, nz)
            for j, gap in ((0, low), (ny - 1, high)):
                line = jnp.sum(rows[pl.ds(j, nx, stride=ny), :] * gap, axis=0, keepdims=True)
                message[k, pl.ds(j, 1)] = message[k, pl.ds(j, 1)] + line


def coef_part(axis, bit, last, mine, theirs, at, union, union_at, weights):
    is_left = (lax.axis_index(axis) & bit) == 0
    next_left = (lax.axis_index(axis) & (2 * bit)) == 0

    def a(k):
        return pick(is_left, mine[at + k], theirs[at + k])

    def b(k):
        return pick(is_left, theirs[at + k], mine[at + k])

    face = 0.5 * (a(7) + b(6))
    for group, scale in enumerate(SCALES):
        a_lr, b_lr = a(2 + group), b(2 + group)
        m = 1.0 / (1.0 / (scale * face) + a(4 + group) + b(group))
        pa, pb = m * a_lr, m * b_lr
        weights[group] = m
        weights[2 + group] = pa
        weights[4 + group] = pb
        out_ll = a(group) - a_lr * pa
        out_rr = b(4 + group) - b_lr * pb
        if last:
            union[union_at + group] = pick(next_left, out_rr, out_ll)
        else:
            union[union_at + group] = out_ll
            union[union_at + 2 + group] = a_lr * pb
            union[union_at + 4 + group] = out_rr
    if last:
        union[union_at + 2] = pick(next_left, b(7), a(6))
    else:
        union[union_at + 6] = a(6)
        union[union_at + 7] = b(7)


def row_part(axis, bit, last, mine, theirs, weights, union, saved, edged=None):
    is_left = (lax.axis_index(axis) & bit) == 0
    next_left = (lax.axis_index(axis) & (2 * bit)) == 0

    def sides(x, y):
        return pick(is_left, x, y), pick(is_left, y, x)

    for c in range(4):
        group = GROUPS[c]
        a_l, b_l = sides(mine[c], theirs[c])
        a_r, b_r = sides(mine[4 + c], theirs[4 + c])
        if edged is not None:
            coef_mine, coef_theirs, missing = edged
            here = (ADVECT * 0.5) * mine[8] * theirs[8 + c]
            there = (ADVECT * 0.5) * theirs[8] * mine[8 + c]
            missing[c] = here
            a_gap, b_gap = sides(here, there)
            ll = pick(is_left, coef_theirs[group], coef_mine[group])
            rr = pick(is_left, coef_mine[4 + group], coef_theirs[4 + group])
            a_lr, b_lr = sides(coef_mine[2 + group], coef_theirs[2 + group])
            a_l = a_l - a_lr * a_gap
            a_r = a_r - rr * a_gap
            b_l = b_l + ll * b_gap
            b_r = b_r + b_lr * b_gap
        d = b_l - a_r
        saved[c] = weights[group] * d
        out_l = a_l + weights[2 + group] * d
        out_r = b_r - weights[4 + group] * d
        if last:
            union[c] = pick(next_left, out_r, out_l)
        else:
            union[c] = out_l
            union[4 + c] = out_r


def coef_kernel(axis, bit, last, mine, theirs, after, union, weights):
    coef_part(axis, bit, last, mine, theirs, 0, union, 0, weights)


def x_merge_kernel(axis, bit, last, edged, mine, theirs, weights, coef_mine, coef_theirs, near, union, saved, missing=None):
    row_part(
        axis, bit, last, mine, theirs, weights, union, saved,
        (coef_mine, coef_theirs, missing) if edged else None,
    )
    if last:
        union[pl.ds(4, 3)] = near[...]


def y_merge_kernel(axis, bit, last, mine, theirs, union, saved, weights):
    coef_part(axis, bit, last, mine, theirs, 8, union, 4 if last else 8, weights)
    row_part(axis, bit, last, mine, theirs, weights, union, saved)


def fluxes(axis, mine, theirs, saved, missing=None):
    index = lax.axis_index(axis)
    bit = lax.axis_size(axis) // 2
    is_left = (index & bit) == 0
    result = []
    face = 0.5 * (mine[6] + theirs[6])
    weight = [
        1.0 / (1.0 / (scale * face) + mine[4 + group] + theirs[4 + group])
        for group, scale in enumerate(SCALES)
    ]
    for c in range(4):
        group = GROUPS[c]
        d = theirs[c] - mine[c]
        flux = weight[group] * pick(is_left, d, -d)
        zero = jnp.zeros_like(flux)
        low = pick(is_left, zero, flux)
        high = pick(is_left, flux, zero)
        this = bit
        for part, weights in saved[::-1]:
            this = this // 2
            flux = part[c] + weights[4 + group] * high + weights[2 + group] * low
            if this == 1 and missing is not None:
                flux = flux - missing[c]
            side = (index & this) == 0
            low, high = pick(side, low, flux), pick(side, flux, high)
        result.append((low, high))
    return result


def local_kernel(source, gap_x, gap_y, ivx, rx, cx, wx, local_t, cx_t, wx_t, scratch):
    _, nx, ny, nz = source.shape
    x_par = lax.rem(lax.axis_index("gx"), 2) == 0
    row = lax.broadcasted_iota(jnp.int32, (ny, nz), 0)

    def right_side(c, i):
        s = source[c, i]
        s = s + pick(row == 0, gap_y[c, pl.ds(i, 1)], 0.0)
        s = s + pick(row == ny - 1, gap_y[4 + c, pl.ds(i, 1)], 0.0)
        if i == 0:
            s = s + pick(x_par, gap_x[c], 0.0)
        if i == nx - 1:
            s = s + pick(x_par, 0.0, gap_x[c])
        return s

    for c in range(4):
        group = GROUPS[c]
        running = right_side(c, 0)
        forward = [running]
        for i in range(1, nx):
            running = right_side(c, i) + rx[group, i - 1] * running
            forward.append(running)
        value = running * ivx[group, nx - 1]
        scratch[c, pl.ds((nx - 1) * ny, ny)] = value
        for i in range(nx - 2, -1, -1):
            value = forward[i] * ivx[group, i] + rx[group, i] * value
            scratch[c, pl.ds(i * ny, ny)] = value
        for j in range(ny):
            local_t[c, j] = scratch[c, pl.ds(j, nx, stride=ny), :]
    for group in range(2):
        c_rows = cx.at[group].reshape(nx * ny, nz)
        w_rows = wx.at[group].reshape(nx * ny, nz)
        for j in range(ny):
            cx_t[group, j] = c_rows[pl.ds(j, nx, stride=ny), :]
            wx_t[group, j] = w_rows[pl.ds(j, nx, stride=ny), :]


def y_start_kernel(stages, *refs):
    mine, theirs, missing = refs[:3]
    parts = refs[3 : 3 + 2 * stages]
    local_t, cx_t, wx_t, cy, wy, coef_y, solved, message, flux_low, flux_high = refs[3 + 2 * stages :]
    _, ny, nx, nz = local_t.shape
    saved = list(zip(parts[::2], parts[1::2]))
    for c, (low, high) in enumerate(fluxes("gx", mine, theirs, saved, missing)):
        flux_low[c] = low
        flux_high[c] = high
    for c in range(4):
        group = GROUPS[c]
        left = right = None
        for j in range(ny):
            low = flux_low[c, pl.ds(j, 1)]
            high = flux_high[c, pl.ds(j, 1)]
            value = local_t[c, j] + (wx_t[group, j] * high - cx_t[group, j] * low)
            solved[c, j] = value
            a, b = cy[group, j] * value, wy[group, j] * value
            left = a if j == 0 else left + a
            right = b if j == 0 else right + b
        message[c] = left
        message[4 + c] = right
    message[pl.ds(8, 8)] = coef_y[...]


def y_local_kernel(solved, ivy, ry, local):
    _, ny, nx, nz = solved.shape
    for c in range(4):
        group = GROUPS[c]
        rows = local.at[c].reshape(nx * ny, nz)
        running = solved[c, 0]
        forward = [running]
        for j in range(1, ny):
            running = solved[c, j] + ry[group, j - 1] * running
            forward.append(running)
        value = running * ivy[group, ny - 1]
        rows[pl.ds(ny - 1, nx, stride=ny), :] = value
        for j in range(ny - 2, -1, -1):
            value = forward[j] * ivy[group, j] + ry[group, j] * value
            rows[pl.ds(j, nx, stride=ny), :] = value


def finish_kernel(stages, *refs):
    mine, theirs = refs[:2]
    parts = refs[2 : 2 + 2 * stages]
    local, cy_t, wy_t, out, buffer, flux_low, flux_high, sems = refs[2 + 2 * stages :]
    saved = list(zip(parts[::2], parts[1::2]))
    nx = local.shape[1]
    for c, (low, high) in enumerate(fluxes("gy", mine, theirs, saved)):
        flux_low[c] = low
        flux_high[c] = high
    copies = []
    for c in range(4):
        group = GROUPS[c]
        for i in range(nx):
            low = flux_low[c, pl.ds(i, 1)]
            high = flux_high[c, pl.ds(i, 1)]
            buffer[c, i] = local[c, i] + (wy_t[group, i] * high - cy_t[group, i] * low)
        copies.append(pltpu.make_async_copy(buffer.at[c], out.at[c], sems.at[c]))
        copies[-1].start()
    for copy in copies:
        copy.wait()


def swap(array, axis, bit):
    return lax.ppermute(array, axis, [(i, i ^ bit) for i in range(lax.axis_size(axis))])


def after_all(spec_count):
    return [VMEM] * spec_count + [pl.BlockSpec(memory_space=pl.ANY)]


def per_device(flow, visc):
    fields, nx, ny, nz = flow.shape
    mx, my = lax.axis_size("gx"), lax.axis_size("gy")
    along_x, along_y = (2, nx, ny, nz), (2, ny, nx, nz)
    x_edge, y_edge_even, y_edge_odd, ivx, rx, cx, wx, coef_x = call(
        first_kernel,
        tuple(pltpu.with_memory_space_constraint(array, pltpu.HBM) for array in (flow, visc)),
        [(fields, ny, nz), (fields, nx, nz), (fields, nx, nz)] + [along_x] * 4 + [(8, ny, nz)],
        scratch=[pltpu.VMEM((nx, ny, nz), F32), pltpu.SemaphoreType.DMA((4,))],
        in_specs=[HBM, HBM],
    )
    pairs = []
    for i in range(mx):
        for j in range(my):
            inner = 0 < i < mx - 1
            partner = ((i - 1 ^ 1) + 1, j) if inner else (i, j ^ 1)
            pairs.append((i * my + j, partner[0] * my + partner[1]))
    x_odd = lax.ppermute(x_edge, ("gx", "gy"), pairs)
    y_odd = lax.ppermute(
        y_edge_odd, "gy", [(i, (i - 1 ^ 1) + 1) if 0 < i < my - 1 else (i, my - 1 - i) for i in range(my)]
    )
    y_even = swap(y_edge_even, "gy", 1)

    ivy, ry, cy, wy, coef_y, cy_t, wy_t = call(
        factor_y_kernel, (visc,), [along_y] * 4 + [(8, nx, nz)] + [along_x] * 2
    )
    coef_x_theirs = swap(coef_x, "gx", 1)
    source, partial = call(source_kernel, (flow, cx, wx), [(fields, nx, ny, nz), (12, ny, nz)])
    message, gap_x, gap_y = call(
        edge_kernel,
        (partial, x_edge, y_edge_even, y_edge_odd, x_odd, y_even, y_odd, cx, wx, coef_x_theirs),
        [(12, ny, nz), (fields, ny, nz), (2 * fields, nx, nz)],
        in_specs=after_all(9),
    )
    local_t, cx_t, wx_t = call(
        local_kernel,
        (source, gap_x, gap_y, ivx, rx, cx, wx),
        [(fields, ny, nx, nz), along_y, along_y],
        scratch=[pltpu.VMEM((fields, nx * ny, nz), F32)],
        cost=1000,
    )

    saved = []
    coefs, coefs_theirs, rows = coef_x, coef_x_theirs, message
    shape = (ny, nz)
    bit = 1
    while 2 * bit < mx:
        last = 4 * bit == mx
        rows_theirs = swap(rows, "gx", bit)
        merged, weights = call(
            functools.partial(coef_kernel, "gx", bit, last),
            (coefs, coefs_theirs, rows),
            [(3 if last else 8,) + shape, (6,) + shape],
            in_specs=after_all(2),
        )
        merged_theirs = merged if last else swap(merged, "gx", 2 * bit)
        rows, part, *gap = call(
            functools.partial(x_merge_kernel, "gx", bit, last, bit == 1),
            (rows, rows_theirs, weights, coefs, coefs_theirs, merged),
            [(7 if last else 8,) + shape, (4,) + shape] + [(4,) + shape] * (bit == 1),
        )
        if gap:
            missing = gap[0]
        saved += [part, weights]
        coefs, coefs_theirs = merged, merged_theirs
        bit *= 2
    rows_theirs = swap(rows, "gx", bit)

    solved, rows = call(
        functools.partial(y_start_kernel, len(saved) // 2),
        (rows, rows_theirs, missing, *saved, local_t, cx_t, wx_t, cy, wy, coef_y),
        [(fields, ny, nx, nz), (16, nx, nz)],
        scratch=[pltpu.VMEM((fields, ny, nz), F32)] * 2,
    )
    (local_y,) = call(y_local_kernel, (solved, ivy, ry), [(fields, nx, ny, nz)])
    saved = []
    shape = (nx, nz)
    bit = 1
    while 2 * bit < my:
        last = 4 * bit == my
        rows, part, weights = call(
            functools.partial(y_merge_kernel, "gy", bit, last),
            (rows, swap(rows, "gy", bit)),
            [(7 if last else 16,) + shape, (4,) + shape, (6,) + shape],
        )
        saved += [part, weights]
        bit *= 2
    rows_theirs = swap(rows, "gy", bit)
    (out,) = call(
        functools.partial(finish_kernel, len(saved) // 2),
        (rows, rows_theirs, *saved, local_y, cy_t, wy_t),
        [(fields, nx, ny, nz)],
        scratch=[
            pltpu.VMEM((fields, nx, ny, nz), F32),
            pltpu.VMEM((fields, nx, nz), F32),
            pltpu.VMEM((fields, nx, nz), F32),
            pltpu.SemaphoreType.DMA((fields,)),
        ],
        out_specs=[HBM],
    )
    return out


def solution(mesh):
    placed = (P(None, "gx", "gy", None), P("gx", "gy", None))
    return jax.shard_map(
        per_device, mesh=mesh, in_specs=placed, out_specs=P(None, "gx", "gy", None), check_vma=False
    )
```

```python
import functools

import jax
import jax.numpy as jnp
from jax import lax
from jax.experimental import pallas as pl
from jax.experimental.pallas import tpu as pltpu
from jax.sharding import PartitionSpec as P

ADVECT = 0.2
BUOYANT = 0.5
CONDUCT = 0.6
GROUPS = (0, 0, 0, 1)
SCALES = (1.0, CONDUCT)
EARLY = 3
VMEM = pl.BlockSpec(memory_space=pltpu.VMEM)
HBM = pl.BlockSpec(memory_space=pltpu.HBM)
F32 = jnp.float32


def call(kernel, ins, outs, scratch=(), in_specs=None, out_specs=None, cost=1000, vmem=40):
    return pl.pallas_call(
        kernel,
        out_shape=[jax.ShapeDtypeStruct(shape, F32) for shape in outs],
        in_specs=in_specs or [VMEM] * len(ins),
        out_specs=out_specs or [VMEM] * len(outs),
        scratch_shapes=list(scratch),
        compiler_params=pltpu.CompilerParams(vmem_limit_bytes=vmem * 1024 * 1024),
        cost_estimate=pl.CostEstimate(flops=cost, bytes_accessed=cost, transcendentals=0),
    )(*ins)


def pick(flag, a, b):
    return jnp.where(flag, a, b)


def factor_line(load, count, first, last, inv, ratio, left, right):
    for group, scale in enumerate(SCALES):
        here = load(0)
        excess = 1.0 + pick(first, scale * here, 0.0)
        column = None
        columns = []
        for i in range(count):
            if i < count - 1:
                beyond = load(i + 1)
                face = (0.5 * scale) * (here + beyond)
                inverse = 1.0 / (excess + face)
                portion = face * inverse
                ratio[group, i] = portion
                inv[group, i] = inverse
                columns.append(column)
                column = portion if column is None else column * portion
                excess = 1.0 + portion * excess
                here = beyond
            else:
                excess = excess + pick(last, scale * here, 0.0)
                inverse = 1.0 / excess
                inv[group, i] = inverse
                ratio[group, i] = inverse
                columns.append(column)
        response = inverse
        onward = column * inverse
        right[group, count - 1] = response
        left[group, count - 1] = onward
        for i in range(count - 2, -1, -1):
            portion = ratio[group, i]
            response = portion * response
            start = inv[group, i] if i == 0 else columns[i] * inv[group, i]
            onward = start + portion * onward
            right[group, i] = response
            left[group, i] = onward


def coef_rows(left, right, out, count):
    for group in range(2):
        out[group] = left[group, 0]
        out[2 + group] = left[group, count - 1]
        out[4 + group] = right[group, count - 1]


def pack_kernel(flow, visc, x_even, x_odd, y_even, y_odd, cells, sems):
    nx, ny = flow.shape[1], flow.shape[2]
    x_par = lax.rem(lax.axis_index("gx"), 2)
    y_par = lax.rem(lax.axis_index("gy"), 2)
    copies = (
        (flow.at[:, x_par * (nx - 1)], x_odd),
        (flow.at[:, :, (1 - y_par) * (ny - 1)], y_even),
        (flow.at[:, :, y_par * (ny - 1)], y_odd),
        (flow.at[:, (1 - x_par) * (nx - 1)], x_even),
        (visc, cells),
    )
    started = [pltpu.make_async_copy(a, b, sems.at[i]) for i, (a, b) in enumerate(copies)]
    for copy in started:
        copy.start()
    for copy in started:
        copy.wait()


def factor_x_kernel(visc, x_even, after, ivx, rx, cx, wx, coef_x):
    nx = visc.shape[0]
    ix = lax.axis_index("gx")
    factor_line(lambda i: visc[i], nx, ix == 0, ix == lax.axis_size("gx") - 1, ivx, rx, cx, wx)
    coef_rows(cx, wx, coef_x, nx)
    coef_x[6] = visc[0]
    coef_x[7] = visc[nx - 1]
    coef_x[pl.ds(8, EARLY)] = x_even[pl.ds(0, EARLY)]


def factor_y_kernel(visc, ivy, ry, cy, wy, coef_y):
    nx, ny, nz = visc.shape
    iy = lax.axis_index("gy")
    rows = visc.reshape(nx * ny, nz)

    def row_y(j):
        return rows[pl.ds(j, nx, stride=ny), :]

    factor_line(row_y, ny, iy == 0, iy == lax.axis_size("gy") - 1, ivy, ry, cy, wy)
    coef_rows(cy, wy, coef_y, ny)
    coef_y[6] = row_y(0)
    coef_y[7] = row_y(ny - 1)


def source_kernel(flow, cx, wx, source, message):
    _, nx, ny, nz = flow.shape
    row = lax.broadcasted_iota(jnp.int32, (ny, nz), 0)
    left = [None] * 4
    right = [None] * 4
    for i in range(nx):
        velocity = [ADVECT * 0.5 * flow[c, i] for c in range(3)]
        for c in range(4):
            f = flow[c, i]
            down = 0.0 if i == 0 else flow[c, i - 1]
            up = 0.0 if i == nx - 1 else flow[c, i + 1]
            below = pick(row == 0, 0.0, pltpu.roll(f, 1, 0))
            above = pick(row == ny - 1, 0.0, pltpu.roll(f, ny - 1, 0))
            z_low = pltpu.roll(f, 1, 1)
            z_high = pltpu.roll(f, nz - 1, 1)
            s = f - (
                velocity[0] * (up - down)
                + velocity[1] * (above - below)
                + velocity[2] * (z_high - z_low)
            )
            if c == 2:
                s = s + BUOYANT * flow[3, i]
            source[c, i] = s
            group = GROUPS[c]
            a, b = cx[group, i] * s, wx[group, i] * s
            left[c] = a if i == 0 else left[c] + a
            right[c] = b if i == 0 else right[c] + b
    for c in range(4):
        message[c] = left[c]
        message[4 + c] = right[c]


def edge_kernel(partial, x_edge_even, x_edge, y_edge_even, y_edge_odd, x_odd, y_even, y_odd, cx, wx, message, gap_x, gap_y):
    _, nx, ny, nz = cx.shape
    ix, iy = lax.axis_index("gx"), lax.axis_index("gy")
    x_par, y_par = lax.rem(ix, 2) == 0, lax.rem(iy, 2) == 0
    x_none = (ix == 0) | (ix == lax.axis_size("gx") - 1)
    y_first, y_last = iy == 0, iy == lax.axis_size("gy") - 1
    half = 0.5 * ADVECT
    own_low = half * pick(y_par, y_edge_odd[1], y_edge_even[1])
    own_high = half * pick(y_par, y_edge_even[1], y_edge_odd[1])
    own_x = half * x_edge[0]
    message[pl.ds(8, 4 - EARLY)] = x_edge_even[pl.ds(EARLY, 4 - EARLY)]
    for c in range(4):
        group = GROUPS[c]
        low = own_low * pick(y_par, y_odd[c], y_even[c])
        high = -own_high * pick(y_par, y_even[c], y_odd[c])
        low = pick(y_first, 0.0, low)
        high = pick(y_last, 0.0, high)
        gap_y[c] = low
        gap_y[4 + c] = high
        across = own_x * x_odd[c]
        across = pick(x_none, 0.0, pick(x_par, across, -across))
        gap_x[c] = across
        for k, part in ((c, cx), (4 + c, wx)):
            edge = pick(x_par, part[group, 0], part[group, nx - 1])
            message[k] = partial[k] + edge * across
            rows = part.at[group].reshape(nx * ny, nz)
            for j, gap in ((0, low), (ny - 1, high)):
                line = jnp.sum(rows[pl.ds(j, nx, stride=ny), :] * gap, axis=0, keepdims=True)
                message[k, pl.ds(j, 1)] = message[k, pl.ds(j, 1)] + line


def coef_part(axis, bit, last, mine, theirs, at, union, union_at, weights):
    is_left = (lax.axis_index(axis) & bit) == 0
    next_left = (lax.axis_index(axis) & (2 * bit)) == 0

    def a(k):
        return pick(is_left, mine[at + k], theirs[at + k])

    def b(k):
        return pick(is_left, theirs[at + k], mine[at + k])

    face = 0.5 * (a(7) + b(6))
    for group, scale in enumerate(SCALES):
        a_lr, b_lr = a(2 + group), b(2 + group)
        m = 1.0 / (1.0 / (scale * face) + a(4 + group) + b(group))
        pa, pb = m * a_lr, m * b_lr
        weights[group] = m
        weights[2 + group] = pa
        weights[4 + group] = pb
        out_ll = a(group) - a_lr * pa
        out_rr = b(4 + group) - b_lr * pb
        if last:
            union[union_at + group] = pick(next_left, out_rr, out_ll)
        else:
            union[union_at + group] = out_ll
            union[union_at + 2 + group] = a_lr * pb
            union[union_at + 4 + group] = out_rr
    if last:
        union[union_at + 2] = pick(next_left, b(7), a(6))
    else:
        union[union_at + 6] = a(6)
        union[union_at + 7] = b(7)


def row_part(axis, bit, last, mine, theirs, weights, union, saved, edged=None):
    is_left = (lax.axis_index(axis) & bit) == 0
    next_left = (lax.axis_index(axis) & (2 * bit)) == 0

    def sides(x, y):
        return pick(is_left, x, y), pick(is_left, y, x)

    for c in range(4):
        group = GROUPS[c]
        a_l, b_l = sides(mine[c], theirs[c])
        a_r, b_r = sides(mine[4 + c], theirs[4 + c])
        if edged is not None:
            coef_mine, coef_theirs, missing = edged
            k = 8 + c if c < EARLY else 8 + c - EARLY
            facing_mine, facing_theirs = (coef_mine, coef_theirs) if c < EARLY else (mine, theirs)
            here = (ADVECT * 0.5) * coef_mine[8] * facing_theirs[k]
            there = (ADVECT * 0.5) * coef_theirs[8] * facing_mine[k]
            missing[c] = here
            a_gap, b_gap = sides(here, there)
            ll = pick(is_left, coef_theirs[group], coef_mine[group])
            rr = pick(is_left, coef_mine[4 + group], coef_theirs[4 + group])
            a_lr, b_lr = sides(coef_mine[2 + group], coef_theirs[2 + group])
            a_l = a_l - a_lr * a_gap
            a_r = a_r - rr * a_gap
            b_l = b_l + ll * b_gap
            b_r = b_r + b_lr * b_gap
        d = b_l - a_r
        saved[c] = weights[group] * d
        out_l = a_l + weights[2 + group] * d
        out_r = b_r - weights[4 + group] * d
        if last:
            union[c] = pick(next_left, out_r, out_l)
        else:
            union[c] = out_l
            union[4 + c] = out_r


def coef_kernel(axis, bit, last, mine, theirs, after, union, weights):
    coef_part(axis, bit, last, mine, theirs, 0, union, 0, weights)
    if last:
        union[3] = union[2]


def x_merge_kernel(axis, bit, last, edged, mine, theirs, weights, coef_mine, coef_theirs, union, saved, missing=None):
    row_part(
        axis, bit, last, mine, theirs, weights, union, saved,
        (coef_mine, coef_theirs, missing) if edged else None,
    )


def last_weight(mine, theirs, at):
    face = 0.5 * (mine[at + 2] + theirs[at + 2])
    return [
        1.0 / (1.0 / (scale * face) + mine[at + group] + theirs[at + group])
        for group, scale in enumerate(SCALES)
    ]


def last_coef_kernel(mine, theirs, weight):
    for group, value in enumerate(last_weight(mine, theirs, 0)):
        weight[group] = value


def y_merge_kernel(axis, bit, last, mine, theirs, union, saved, weights):
    coef_part(axis, bit, last, mine, theirs, 8, union, 4 if last else 8, weights)
    row_part(axis, bit, last, mine, theirs, weights, union, saved)


def fluxes(axis, mine, theirs, weight, saved, missing=None):
    index = lax.axis_index(axis)
    bit = lax.axis_size(axis) // 2
    is_left = (index & bit) == 0
    result = []
    for c in range(4):
        group = GROUPS[c]
        d = theirs[c] - mine[c]
        flux = weight[group] * pick(is_left, d, -d)
        zero = jnp.zeros_like(flux)
        low = pick(is_left, zero, flux)
        high = pick(is_left, flux, zero)
        this = bit
        for part, weights in saved[::-1]:
            this = this // 2
            flux = part[c] + weights[4 + group] * high + weights[2 + group] * low
            if this == 1 and missing is not None:
                flux = flux - missing[c]
            side = (index & this) == 0
            low, high = pick(side, low, flux), pick(side, flux, high)
        result.append((low, high))
    return result


def local_kernel(source, gap_x, gap_y, ivx, rx, cx, wx, after, local_t, cx_t, wx_t, scratch):
    _, nx, ny, nz = source.shape
    x_par = lax.rem(lax.axis_index("gx"), 2) == 0
    row = lax.broadcasted_iota(jnp.int32, (ny, nz), 0)

    def right_side(c, i):
        s = source[c, i]
        s = s + pick(row == 0, gap_y[c, pl.ds(i, 1)], 0.0)
        s = s + pick(row == ny - 1, gap_y[4 + c, pl.ds(i, 1)], 0.0)
        if i == 0:
            s = s + pick(x_par, gap_x[c], 0.0)
        if i == nx - 1:
            s = s + pick(x_par, 0.0, gap_x[c])
        return s

    for c in range(4):
        group = GROUPS[c]
        running = right_side(c, 0)
        forward = [running]
        for i in range(1, nx):
            running = right_side(c, i) + rx[group, i - 1] * running
            forward.append(running)
        value = running * ivx[group, nx - 1]
        scratch[c, pl.ds((nx - 1) * ny, ny)] = value
        for i in range(nx - 2, -1, -1):
            value = forward[i] * ivx[group, i] + rx[group, i] * value
            scratch[c, pl.ds(i * ny, ny)] = value
        for j in range(ny):
            local_t[c, j] = scratch[c, pl.ds(j, nx, stride=ny), :]
    for group in range(2):
        c_rows = cx.at[group].reshape(nx * ny, nz)
        w_rows = wx.at[group].reshape(nx * ny, nz)
        for j in range(ny):
            cx_t[group, j] = c_rows[pl.ds(j, nx, stride=ny), :]
            wx_t[group, j] = w_rows[pl.ds(j, nx, stride=ny), :]


def y_start_kernel(stages, *refs):
    mine, theirs, weight, missing = refs[:4]
    parts = refs[4 : 4 + 2 * stages]
    local_t, cx_t, wx_t, cy, wy, coef_y, solved, message, flux_low, flux_high = refs[4 + 2 * stages :]
    _, ny, nx, nz = local_t.shape
    saved = list(zip(parts[::2], parts[1::2]))
    for c, (low, high) in enumerate(fluxes("gx", mine, theirs, weight, saved, missing)):
        flux_low[c] = low
        flux_high[c] = high
    for c in range(4):
        group = GROUPS[c]
        left = right = None
        for j in range(ny):
            low = flux_low[c, pl.ds(j, 1)]
            high = flux_high[c, pl.ds(j, 1)]
            value = local_t[c, j] + (wx_t[group, j] * high - cx_t[group, j] * low)
            solved[c, j] = value
            a, b = cy[group, j] * value, wy[group, j] * value
            left = a if j == 0 else left + a
            right = b if j == 0 else right + b
        message[c] = left
        message[4 + c] = right
    message[pl.ds(8, 8)] = coef_y[...]


def y_local_kernel(solved, ivy, ry, cy, wy, local, cy_t, wy_t):
    _, ny, nx, nz = solved.shape
    for part, turned in ((cy, cy_t), (wy, wy_t)):
        for group in range(2):
            out = turned.at[group].reshape(nx * ny, nz)
            for j in range(ny):
                out[pl.ds(j, nx, stride=ny), :] = part[group, j]
    for c in range(4):
        group = GROUPS[c]
        rows = local.at[c].reshape(nx * ny, nz)
        running = solved[c, 0]
        forward = [running]
        for j in range(1, ny):
            running = solved[c, j] + ry[group, j - 1] * running
            forward.append(running)
        value = running * ivy[group, ny - 1]
        rows[pl.ds(ny - 1, nx, stride=ny), :] = value
        for j in range(ny - 2, -1, -1):
            value = forward[j] * ivy[group, j] + ry[group, j] * value
            rows[pl.ds(j, nx, stride=ny), :] = value


def finish_kernel(stages, *refs):
    mine, theirs = refs[:2]
    parts = refs[2 : 2 + 2 * stages]
    local, cy_t, wy_t, out, buffer, flux_low, flux_high, sems = refs[2 + 2 * stages :]
    saved = list(zip(parts[::2], parts[1::2]))
    nx = local.shape[1]
    for c, (low, high) in enumerate(fluxes("gy", mine, theirs, last_weight(mine, theirs, 4), saved)):
        flux_low[c] = low
        flux_high[c] = high
    copies = []
    for c in range(4):
        group = GROUPS[c]
        for i in range(nx):
            low = flux_low[c, pl.ds(i, 1)]
            high = flux_high[c, pl.ds(i, 1)]
            buffer[c, i] = local[c, i] + (wy_t[group, i] * high - cy_t[group, i] * low)
        copies.append(pltpu.make_async_copy(buffer.at[c], out.at[c], sems.at[c]))
        copies[-1].start()
    for copy in copies:
        copy.wait()


def swap(array, axis, bit):
    return lax.ppermute(array, axis, [(i, i ^ bit) for i in range(lax.axis_size(axis))])


def after_all(spec_count):
    return [VMEM] * spec_count + [pl.BlockSpec(memory_space=pl.ANY)]


def per_device(flow, visc):
    fields, nx, ny, nz = flow.shape
    mx, my = lax.axis_size("gx"), lax.axis_size("gy")
    along_x, along_y = (2, nx, ny, nz), (2, ny, nx, nz)
    along_x, along_y = (2, nx, ny, nz), (2, ny, nx, nz)
    x_edge_even, x_edge, y_edge_even, y_edge_odd, cells = call(
        pack_kernel,
        tuple(pltpu.with_memory_space_constraint(array, pltpu.HBM) for array in (flow, visc)),
        [(fields, ny, nz)] * 2 + [(fields, nx, nz)] * 2 + [(nx, ny, nz)],
        scratch=[pltpu.SemaphoreType.DMA((5,))],
        in_specs=[HBM, HBM],
    )
    pairs = []
    for i in range(mx):
        for j in range(my):
            inner = 0 < i < mx - 1
            partner = ((i - 1 ^ 1) + 1, j) if inner else (i, j ^ 1)
            pairs.append((i * my + j, partner[0] * my + partner[1]))
    x_odd = lax.ppermute(x_edge, ("gx", "gy"), pairs)
    y_odd = lax.ppermute(
        y_edge_odd, "gy", [(i, (i - 1 ^ 1) + 1) if 0 < i < my - 1 else (i, my - 1 - i) for i in range(my)]
    )
    y_even = swap(y_edge_even, "gy", 1)
    ivx, rx, cx, wx, coef_x = call(
        factor_x_kernel,
        (cells, x_edge_even, y_even),
        [along_x] * 4 + [(8 + EARLY, ny, nz)],
        in_specs=after_all(2),
    )

    ivy, ry, cy, wy, coef_y = call(factor_y_kernel, (cells,), [along_y] * 4 + [(8, nx, nz)])
    coef_x_theirs = swap(coef_x, "gx", 1)
    source, partial = call(source_kernel, (flow, cx, wx), [(fields, nx, ny, nz), (8, ny, nz)])
    message, gap_x, gap_y = call(
        edge_kernel,
        (partial, x_edge_even, x_edge, y_edge_even, y_edge_odd, x_odd, y_even, y_odd, cx, wx),
        [(12 - EARLY, ny, nz), (fields, ny, nz), (2 * fields, nx, nz)],
    )
    local_t, cx_t, wx_t = call(
        local_kernel,
        (source, gap_x, gap_y, ivx, rx, cx, wx, ivy),
        in_specs=after_all(7),
        outs=[(fields, ny, nx, nz), along_y, along_y],
        scratch=[pltpu.VMEM((fields, nx * ny, nz), F32)],
        cost=1000,
    )

    saved = []
    coefs, coefs_theirs, rows = coef_x, coef_x_theirs, message
    shape = (ny, nz)
    bit = 1
    while 2 * bit < mx:
        last = 4 * bit == mx
        rows_theirs = swap(rows, "gx", bit)
        merged, weights = call(
            functools.partial(coef_kernel, "gx", bit, last),
            (coefs, coefs_theirs, local_t if bit == 1 else rows),
            [(4 if last else 8,) + shape, (6,) + shape],
            in_specs=after_all(2),
        )
        merged_theirs = swap(merged, "gx", 2 * bit)
        rows, part, *gap = call(
            functools.partial(x_merge_kernel, "gx", bit, last, bit == 1),
            (rows, rows_theirs, weights, coefs, coefs_theirs),
            [(4 if last else 8,) + shape, (4,) + shape] + [(4,) + shape] * (bit == 1),
        )
        if gap:
            missing = gap[0]
        saved += [part, weights]
        coefs, coefs_theirs = merged, merged_theirs
        bit *= 2
    rows_theirs = swap(rows, "gx", bit)

    (weight,) = call(last_coef_kernel, (coefs, coefs_theirs), [(2, ny, nz)])
    solved, rows = call(
        functools.partial(y_start_kernel, len(saved) // 2),
        (rows, rows_theirs, weight, missing, *saved, local_t, cx_t, wx_t, cy, wy, coef_y),
        [(fields, ny, nx, nz), (16, nx, nz)],
        scratch=[pltpu.VMEM((fields, ny, nz), F32)] * 2,
    )
    local_y, cy_t, wy_t = call(
        y_local_kernel, (solved, ivy, ry, cy, wy), [(fields, nx, ny, nz), along_x, along_x]
    )
    saved = []
    shape = (nx, nz)
    bit = 1
    while 2 * bit < my:
        last = 4 * bit == my
        rows, part, weights = call(
            functools.partial(y_merge_kernel, "gy", bit, last),
            (rows, swap(rows, "gy", bit)),
            [(7 if last else 16,) + shape, (4,) + shape, (6,) + shape],
        )
        saved += [part, weights]
        bit *= 2
    rows_theirs = swap(rows, "gy", bit)
    (out,) = call(
        functools.partial(finish_kernel, len(saved) // 2),
        (rows, rows_theirs, *saved, local_y, cy_t, wy_t),
        [(fields, nx, ny, nz)],
        scratch=[
            pltpu.VMEM((fields, nx, ny, nz), F32),
            pltpu.VMEM((fields, nx, nz), F32),
            pltpu.VMEM((fields, nx, nz), F32),
            pltpu.SemaphoreType.DMA((fields,)),
        ],
        out_specs=[HBM],
    )
    return out


def solution(mesh):
    placed = (P(None, "gx", "gy", None), P("gx", "gy", None))
    return jax.shard_map(
        per_device, mesh=mesh, in_specs=placed, out_specs=P(None, "gx", "gy", None), check_vma=False
    )
```

```python
import functools

import jax
import jax.numpy as jnp
from jax import lax
from jax.experimental import pallas as pl
from jax.experimental.pallas import tpu as pltpu
from jax.sharding import PartitionSpec as P

ADVECT = 0.2
BUOYANT = 0.5
CONDUCT = 0.6
GROUPS = (0, 0, 0, 1)
SCALES = (1.0, CONDUCT)
EARLY = 3
VMEM = pl.BlockSpec(memory_space=pltpu.VMEM)
HBM = pl.BlockSpec(memory_space=pltpu.HBM)
F32 = jnp.float32


def call(kernel, ins, outs, scratch=(), in_specs=None, out_specs=None, cost=1000, vmem=40):
    return pl.pallas_call(
        kernel,
        out_shape=[jax.ShapeDtypeStruct(shape, F32) for shape in outs],
        in_specs=in_specs or [VMEM] * len(ins),
        out_specs=out_specs or [VMEM] * len(outs),
        scratch_shapes=list(scratch),
        compiler_params=pltpu.CompilerParams(vmem_limit_bytes=vmem * 1024 * 1024),
        cost_estimate=pl.CostEstimate(flops=cost, bytes_accessed=cost, transcendentals=0),
    )(*ins)


def pick(flag, a, b):
    return jnp.where(flag, a, b)


def factor_line(load, count, first, last, inv, ratio, left, right):
    for group, scale in enumerate(SCALES):
        here = load(0)
        excess = 1.0 + pick(first, scale * here, 0.0)
        column = None
        columns = []
        for i in range(count):
            if i < count - 1:
                beyond = load(i + 1)
                face = (0.5 * scale) * (here + beyond)
                inverse = 1.0 / (excess + face)
                portion = face * inverse
                ratio[group, i] = portion
                inv[group, i] = inverse
                columns.append(column)
                column = portion if column is None else column * portion
                excess = 1.0 + portion * excess
                here = beyond
            else:
                excess = excess + pick(last, scale * here, 0.0)
                inverse = 1.0 / excess
                inv[group, i] = inverse
                ratio[group, i] = inverse
                columns.append(column)
        response = inverse
        onward = column * inverse
        right[group, count - 1] = response
        left[group, count - 1] = onward
        for i in range(count - 2, -1, -1):
            portion = ratio[group, i]
            response = portion * response
            start = inv[group, i] if i == 0 else columns[i] * inv[group, i]
            onward = start + portion * onward
            right[group, i] = response
            left[group, i] = onward


def coef_rows(left, right, out, count):
    for group in range(2):
        out[group] = left[group, 0]
        out[2 + group] = left[group, count - 1]
        out[4 + group] = right[group, count - 1]


def pack_kernel(flow, visc, x_odd, y_even, y_odd, cells, sems):
    nx, ny = flow.shape[1], flow.shape[2]
    x_par = lax.rem(lax.axis_index("gx"), 2)
    y_par = lax.rem(lax.axis_index("gy"), 2)
    copies = (
        (flow.at[:, x_par * (nx - 1)], x_odd),
        (flow.at[:, :, (1 - y_par) * (ny - 1)], y_even),
        (flow.at[:, :, y_par * (ny - 1)], y_odd),
        (visc, cells),
    )
    started = [pltpu.make_async_copy(a, b, sems.at[i]) for i, (a, b) in enumerate(copies)]
    for copy in started:
        copy.start()
    for copy in started:
        copy.wait()


def factor_x_kernel(visc, flow, after, ivx, rx, cx, wx, coef_x, x_even):
    nx = visc.shape[0]
    ix = lax.axis_index("gx")
    factor_line(lambda i: visc[i], nx, ix == 0, ix == lax.axis_size("gx") - 1, ivx, rx, cx, wx)
    coef_rows(cx, wx, coef_x, nx)
    coef_x[6] = visc[0]
    coef_x[7] = visc[nx - 1]
    for c in range(4):
        facing = pick(lax.rem(ix, 2) == 0, flow[c, nx - 1], flow[c, 0])
        if c < EARLY:
            coef_x[8 + c] = facing
        x_even[c] = facing


def factor_y_kernel(visc, ivy, ry, cy, wy, coef_y):
    nx, ny, nz = visc.shape
    iy = lax.axis_index("gy")
    rows = visc.reshape(nx * ny, nz)

    def row_y(j):
        return rows[pl.ds(j, nx, stride=ny), :]

    factor_line(row_y, ny, iy == 0, iy == lax.axis_size("gy") - 1, ivy, ry, cy, wy)
    coef_rows(cy, wy, coef_y, ny)
    coef_y[6] = row_y(0)
    coef_y[7] = row_y(ny - 1)


def source_kernel(flow, cx, wx, source, message):
    _, nx, ny, nz = flow.shape
    row = lax.broadcasted_iota(jnp.int32, (ny, nz), 0)
    left = [None] * 4
    right = [None] * 4
    for i in range(nx):
        velocity = [ADVECT * 0.5 * flow[c, i] for c in range(3)]
        for c in range(4):
            f = flow[c, i]
            down = 0.0 if i == 0 else flow[c, i - 1]
            up = 0.0 if i == nx - 1 else flow[c, i + 1]
            below = pick(row == 0, 0.0, pltpu.roll(f, 1, 0))
            above = pick(row == ny - 1, 0.0, pltpu.roll(f, ny - 1, 0))
            z_low = pltpu.roll(f, 1, 1)
            z_high = pltpu.roll(f, nz - 1, 1)
            s = f - (
                velocity[0] * (up - down)
                + velocity[1] * (above - below)
                + velocity[2] * (z_high - z_low)
            )
            if c == 2:
                s = s + BUOYANT * flow[3, i]
            source[c, i] = s
            group = GROUPS[c]
            a, b = cx[group, i] * s, wx[group, i] * s
            left[c] = a if i == 0 else left[c] + a
            right[c] = b if i == 0 else right[c] + b
    for c in range(4):
        message[c] = left[c]
        message[4 + c] = right[c]


def edge_kernel(partial, x_edge_even, x_edge, y_edge_even, y_edge_odd, x_odd, y_even, y_odd, cx, wx, after, message, gap_x, gap_y):
    _, nx, ny, nz = cx.shape
    ix, iy = lax.axis_index("gx"), lax.axis_index("gy")
    x_par, y_par = lax.rem(ix, 2) == 0, lax.rem(iy, 2) == 0
    x_none = (ix == 0) | (ix == lax.axis_size("gx") - 1)
    y_first, y_last = iy == 0, iy == lax.axis_size("gy") - 1
    half = 0.5 * ADVECT
    own_low = half * pick(y_par, y_edge_odd[1], y_edge_even[1])
    own_high = half * pick(y_par, y_edge_even[1], y_edge_odd[1])
    own_x = half * x_edge[0]
    message[pl.ds(8, 4 - EARLY)] = x_edge_even[pl.ds(EARLY, 4 - EARLY)]
    for c in range(4):
        group = GROUPS[c]
        low = own_low * pick(y_par, y_odd[c], y_even[c])
        high = -own_high * pick(y_par, y_even[c], y_odd[c])
        low = pick(y_first, 0.0, low)
        high = pick(y_last, 0.0, high)
        gap_y[c] = low
        gap_y[4 + c] = high
        across = own_x * x_odd[c]
        across = pick(x_none, 0.0, pick(x_par, across, -across))
        gap_x[c] = across
        for k, part in ((c, cx), (4 + c, wx)):
            edge = pick(x_par, part[group, 0], part[group, nx - 1])
            message[k] = partial[k] + edge * across
            rows = part.at[group].reshape(nx * ny, nz)
            for j, gap in ((0, low), (ny - 1, high)):
                line = jnp.sum(rows[pl.ds(j, nx, stride=ny), :] * gap, axis=0, keepdims=True)
                message[k, pl.ds(j, 1)] = message[k, pl.ds(j, 1)] + line


def coef_part(axis, bit, last, mine, theirs, at, union, union_at, weights):
    is_left = (lax.axis_index(axis) & bit) == 0
    next_left = (lax.axis_index(axis) & (2 * bit)) == 0

    def a(k):
        return pick(is_left, mine[at + k], theirs[at + k])

    def b(k):
        return pick(is_left, theirs[at + k], mine[at + k])

    face = 0.5 * (a(7) + b(6))
    for group, scale in enumerate(SCALES):
        a_lr, b_lr = a(2 + group), b(2 + group)
        m = 1.0 / (1.0 / (scale * face) + a(4 + group) + b(group))
        pa, pb = m * a_lr, m * b_lr
        weights[group] = m
        weights[2 + group] = pa
        weights[4 + group] = pb
        out_ll = a(group) - a_lr * pa
        out_rr = b(4 + group) - b_lr * pb
        if last:
            union[union_at + group] = pick(next_left, out_rr, out_ll)
        else:
            union[union_at + group] = out_ll
            union[union_at + 2 + group] = a_lr * pb
            union[union_at + 4 + group] = out_rr
    if last:
        union[union_at + 2] = pick(next_left, b(7), a(6))
    else:
        union[union_at + 6] = a(6)
        union[union_at + 7] = b(7)


def row_part(axis, bit, last, mine, theirs, weights, union, saved, edged=None):
    is_left = (lax.axis_index(axis) & bit) == 0
    next_left = (lax.axis_index(axis) & (2 * bit)) == 0

    def sides(x, y):
        return pick(is_left, x, y), pick(is_left, y, x)

    for c in range(4):
        group = GROUPS[c]
        a_l, b_l = sides(mine[c], theirs[c])
        a_r, b_r = sides(mine[4 + c], theirs[4 + c])
        if edged is not None:
            coef_mine, coef_theirs, missing = edged
            k = 8 + c if c < EARLY else 8 + c - EARLY
            facing_mine, facing_theirs = (coef_mine, coef_theirs) if c < EARLY else (mine, theirs)
            here = (ADVECT * 0.5) * coef_mine[8] * facing_theirs[k]
            there = (ADVECT * 0.5) * coef_theirs[8] * facing_mine[k]
            missing[c] = here
            a_gap, b_gap = sides(here, there)
            ll = pick(is_left, coef_theirs[group], coef_mine[group])
            rr = pick(is_left, coef_mine[4 + group], coef_theirs[4 + group])
            a_lr, b_lr = sides(coef_mine[2 + group], coef_theirs[2 + group])
            a_l = a_l - a_lr * a_gap
            a_r = a_r - rr * a_gap
            b_l = b_l + ll * b_gap
            b_r = b_r + b_lr * b_gap
        d = b_l - a_r
        saved[c] = weights[group] * d
        out_l = a_l + weights[2 + group] * d
        out_r = b_r - weights[4 + group] * d
        if last:
            union[c] = pick(next_left, out_r, out_l)
        else:
            union[c] = out_l
            union[4 + c] = out_r


def coef_kernel(axis, bit, last, mine, theirs, after, union, weights):
    coef_part(axis, bit, last, mine, theirs, 0, union, 0, weights)
    if last:
        union[3] = union[2]


def x_merge_kernel(axis, bit, last, edged, mine, theirs, weights, coef_mine, coef_theirs, union, saved, missing=None):
    row_part(
        axis, bit, last, mine, theirs, weights, union, saved,
        (coef_mine, coef_theirs, missing) if edged else None,
    )


def last_weight(mine, theirs, at):
    face = 0.5 * (mine[at + 2] + theirs[at + 2])
    return [
        1.0 / (1.0 / (scale * face) + mine[at + group] + theirs[at + group])
        for group, scale in enumerate(SCALES)
    ]


def last_coef_kernel(mine, theirs, weight):
    for group, value in enumerate(last_weight(mine, theirs, 0)):
        weight[group] = value


def y_merge_kernel(axis, bit, last, mine, theirs, union, saved, weights):
    coef_part(axis, bit, last, mine, theirs, 8, union, 4 if last else 8, weights)
    row_part(axis, bit, last, mine, theirs, weights, union, saved)


def fluxes(axis, mine, theirs, weight, saved, missing=None):
    index = lax.axis_index(axis)
    bit = lax.axis_size(axis) // 2
    is_left = (index & bit) == 0
    result = []
    for c in range(4):
        group = GROUPS[c]
        d = theirs[c] - mine[c]
        flux = weight[group] * pick(is_left, d, -d)
        zero = jnp.zeros_like(flux)
        low = pick(is_left, zero, flux)
        high = pick(is_left, flux, zero)
        this = bit
        for part, weights in saved[::-1]:
            this = this // 2
            flux = part[c] + weights[4 + group] * high + weights[2 + group] * low
            if this == 1 and missing is not None:
                flux = flux - missing[c]
            side = (index & this) == 0
            low, high = pick(side, low, flux), pick(side, flux, high)
        result.append((low, high))
    return result


def local_kernel(source, gap_x, gap_y, ivx, rx, cx, wx, local_t, cx_t, wx_t, scratch):
    _, nx, ny, nz = source.shape
    x_par = lax.rem(lax.axis_index("gx"), 2) == 0
    row = lax.broadcasted_iota(jnp.int32, (ny, nz), 0)

    def right_side(c, i):
        s = source[c, i]
        s = s + pick(row == 0, gap_y[c, pl.ds(i, 1)], 0.0)
        s = s + pick(row == ny - 1, gap_y[4 + c, pl.ds(i, 1)], 0.0)
        if i == 0:
            s = s + pick(x_par, gap_x[c], 0.0)
        if i == nx - 1:
            s = s + pick(x_par, 0.0, gap_x[c])
        return s

    for c in range(4):
        group = GROUPS[c]
        running = right_side(c, 0)
        forward = [running]
        for i in range(1, nx):
            running = right_side(c, i) + rx[group, i - 1] * running
            forward.append(running)
        value = running * ivx[group, nx - 1]
        scratch[c, pl.ds((nx - 1) * ny, ny)] = value
        for i in range(nx - 2, -1, -1):
            value = forward[i] * ivx[group, i] + rx[group, i] * value
            scratch[c, pl.ds(i * ny, ny)] = value
        for j in range(ny):
            local_t[c, j] = scratch[c, pl.ds(j, nx, stride=ny), :]
    for group in range(2):
        c_rows = cx.at[group].reshape(nx * ny, nz)
        w_rows = wx.at[group].reshape(nx * ny, nz)
        for j in range(ny):
            cx_t[group, j] = c_rows[pl.ds(j, nx, stride=ny), :]
            wx_t[group, j] = w_rows[pl.ds(j, nx, stride=ny), :]


def y_start_kernel(stages, *refs):
    mine, theirs, weight, missing = refs[:4]
    parts = refs[4 : 4 + 2 * stages]
    local_t, cx_t, wx_t, cy, wy, coef_y, solved, message, flux_low, flux_high = refs[4 + 2 * stages :]
    _, ny, nx, nz = local_t.shape
    saved = list(zip(parts[::2], parts[1::2]))
    for c, (low, high) in enumerate(fluxes("gx", mine, theirs, weight, saved, missing)):
        flux_low[c] = low
        flux_high[c] = high
    for c in range(4):
        group = GROUPS[c]
        left = right = None
        for j in range(ny):
            low = flux_low[c, pl.ds(j, 1)]
            high = flux_high[c, pl.ds(j, 1)]
            value = local_t[c, j] + (wx_t[group, j] * high - cx_t[group, j] * low)
            solved[c, j] = value
            a, b = cy[group, j] * value, wy[group, j] * value
            left = a if j == 0 else left + a
            right = b if j == 0 else right + b
        message[c] = left
        message[4 + c] = right
    message[pl.ds(8, 8)] = coef_y[...]


def y_local_kernel(solved, ivy, ry, cy, wy, local, cy_t, wy_t):
    _, ny, nx, nz = solved.shape
    for part, turned in ((cy, cy_t), (wy, wy_t)):
        for group in range(2):
            out = turned.at[group].reshape(nx * ny, nz)
            for j in range(ny):
                out[pl.ds(j, nx, stride=ny), :] = part[group, j]
    for c in range(4):
        group = GROUPS[c]
        rows = local.at[c].reshape(nx * ny, nz)
        running = solved[c, 0]
        forward = [running]
        for j in range(1, ny):
            running = solved[c, j] + ry[group, j - 1] * running
            forward.append(running)
        value = running * ivy[group, ny - 1]
        rows[pl.ds(ny - 1, nx, stride=ny), :] = value
        for j in range(ny - 2, -1, -1):
            value = forward[j] * ivy[group, j] + ry[group, j] * value
            rows[pl.ds(j, nx, stride=ny), :] = value


def finish_kernel(stages, *refs):
    mine, theirs = refs[:2]
    parts = refs[2 : 2 + 2 * stages]
    local, cy_t, wy_t, out, buffer, flux_low, flux_high, sems = refs[2 + 2 * stages :]
    saved = list(zip(parts[::2], parts[1::2]))
    nx = local.shape[1]
    for c, (low, high) in enumerate(fluxes("gy", mine, theirs, last_weight(mine, theirs, 4), saved)):
        flux_low[c] = low
        flux_high[c] = high
    copies = []
    for c in range(4):
        group = GROUPS[c]
        for i in range(nx):
            low = flux_low[c, pl.ds(i, 1)]
            high = flux_high[c, pl.ds(i, 1)]
            buffer[c, i] = local[c, i] + (wy_t[group, i] * high - cy_t[group, i] * low)
        copies.append(pltpu.make_async_copy(buffer.at[c], out.at[c], sems.at[c]))
        copies[-1].start()
    for copy in copies:
        copy.wait()


def swap(array, axis, bit):
    return lax.ppermute(array, axis, [(i, i ^ bit) for i in range(lax.axis_size(axis))])


def after_all(spec_count):
    return [VMEM] * spec_count + [pl.BlockSpec(memory_space=pl.ANY)]


def per_device(flow, visc):
    fields, nx, ny, nz = flow.shape
    mx, my = lax.axis_size("gx"), lax.axis_size("gy")
    along_x, along_y = (2, nx, ny, nz), (2, ny, nx, nz)
    along_x, along_y = (2, nx, ny, nz), (2, ny, nx, nz)
    x_edge, y_edge_even, y_edge_odd, cells = call(
        pack_kernel,
        tuple(pltpu.with_memory_space_constraint(array, pltpu.HBM) for array in (flow, visc)),
        [(fields, ny, nz)] + [(fields, nx, nz)] * 2 + [(nx, ny, nz)],
        scratch=[pltpu.SemaphoreType.DMA((4,))],
        in_specs=[HBM, HBM],
    )
    pairs = []
    for i in range(mx):
        for j in range(my):
            inner = 0 < i < mx - 1
            partner = ((i - 1 ^ 1) + 1, j) if inner else (i, j ^ 1)
            pairs.append((i * my + j, partner[0] * my + partner[1]))
    x_odd = lax.ppermute(x_edge, ("gx", "gy"), pairs)
    y_odd = lax.ppermute(
        y_edge_odd, "gy", [(i, (i - 1 ^ 1) + 1) if 0 < i < my - 1 else (i, my - 1 - i) for i in range(my)]
    )
    y_even = swap(y_edge_even, "gy", 1)
    ivx, rx, cx, wx, coef_x, x_edge_even = call(
        factor_x_kernel,
        (cells, flow, y_even),
        [along_x] * 4 + [(8 + EARLY, ny, nz), (fields, ny, nz)],
        in_specs=after_all(2),
    )

    ivy, ry, cy, wy, coef_y = call(factor_y_kernel, (cells,), [along_y] * 4 + [(8, nx, nz)])
    coef_x_theirs = swap(coef_x, "gx", 1)
    source, partial = call(source_kernel, (flow, cx, wx), [(fields, nx, ny, nz), (8, ny, nz)])
    message, gap_x, gap_y = call(
        edge_kernel,
        (partial, x_edge_even, x_edge, y_edge_even, y_edge_odd, x_odd, y_even, y_odd, cx, wx, ivy),
        [(12 - EARLY, ny, nz), (fields, ny, nz), (2 * fields, nx, nz)],
        in_specs=after_all(10),
    )
    local_t, cx_t, wx_t = call(
        local_kernel,
        (source, gap_x, gap_y, ivx, rx, cx, wx),
        outs=[(fields, ny, nx, nz), along_y, along_y],
        scratch=[pltpu.VMEM((fields, nx * ny, nz), F32)],
        cost=1000,
    )

    saved = []
    coefs, coefs_theirs, rows = coef_x, coef_x_theirs, message
    shape = (ny, nz)
    bit = 1
    while 2 * bit < mx:
        last = 4 * bit == mx
        rows_theirs = swap(rows, "gx", bit)
        merged, weights = call(
            functools.partial(coef_kernel, "gx", bit, last),
            (coefs, coefs_theirs, local_t if bit == 1 else rows),
            [(4 if last else 8,) + shape, (6,) + shape],
            in_specs=after_all(2),
        )
        merged_theirs = swap(merged, "gx", 2 * bit)
        rows, part, *gap = call(
            functools.partial(x_merge_kernel, "gx", bit, last, bit == 1),
            (rows, rows_theirs, weights, coefs, coefs_theirs),
            [(4 if last else 8,) + shape, (4,) + shape] + [(4,) + shape] * (bit == 1),
        )
        if gap:
            missing = gap[0]
        saved += [part, weights]
        coefs, coefs_theirs = merged, merged_theirs
        bit *= 2
    rows_theirs = swap(rows, "gx", bit)

    (weight,) = call(last_coef_kernel, (coefs, coefs_theirs), [(2, ny, nz)])
    solved, rows = call(
        functools.partial(y_start_kernel, len(saved) // 2),
        (rows, rows_theirs, weight, missing, *saved, local_t, cx_t, wx_t, cy, wy, coef_y),
        [(fields, ny, nx, nz), (16, nx, nz)],
        scratch=[pltpu.VMEM((fields, ny, nz), F32)] * 2,
    )
    local_y, cy_t, wy_t = call(
        y_local_kernel, (solved, ivy, ry, cy, wy), [(fields, nx, ny, nz), along_x, along_x]
    )
    saved = []
    shape = (nx, nz)
    bit = 1
    while 2 * bit < my:
        last = 4 * bit == my
        rows, part, weights = call(
            functools.partial(y_merge_kernel, "gy", bit, last),
            (rows, swap(rows, "gy", bit)),
            [(7 if last else 16,) + shape, (4,) + shape, (6,) + shape],
        )
        saved += [part, weights]
        bit *= 2
    rows_theirs = swap(rows, "gy", bit)
    (out,) = call(
        functools.partial(finish_kernel, len(saved) // 2),
        (rows, rows_theirs, *saved, local_y, cy_t, wy_t),
        [(fields, nx, ny, nz)],
        scratch=[
            pltpu.VMEM((fields, nx, ny, nz), F32),
            pltpu.VMEM((fields, nx, nz), F32),
            pltpu.VMEM((fields, nx, nz), F32),
            pltpu.SemaphoreType.DMA((fields,)),
        ],
        out_specs=[HBM],
    )
    return out


def solution(mesh):
    placed = (P(None, "gx", "gy", None), P("gx", "gy", None))
    return jax.shard_map(
        per_device, mesh=mesh, in_specs=placed, out_specs=P(None, "gx", "gy", None), check_vma=False
    )
```

```python
import functools

import jax
import jax.numpy as jnp
from jax import lax
from jax.experimental import pallas as pl
from jax.experimental.pallas import tpu as pltpu
from jax.sharding import PartitionSpec as P

ADVECT = 0.2
BUOYANT = 0.5
CONDUCT = 0.6
GROUPS = (0, 0, 0, 1)
SCALES = (1.0, CONDUCT)
EARLY = 3
VMEM = pl.BlockSpec(memory_space=pltpu.VMEM)
HBM = pl.BlockSpec(memory_space=pltpu.HBM)
F32 = jnp.float32


def call(kernel, ins, outs, scratch=(), in_specs=None, out_specs=None, cost=1000, vmem=40):
    return pl.pallas_call(
        kernel,
        out_shape=[jax.ShapeDtypeStruct(shape, F32) for shape in outs],
        in_specs=in_specs or [VMEM] * len(ins),
        out_specs=out_specs or [VMEM] * len(outs),
        scratch_shapes=list(scratch),
        compiler_params=pltpu.CompilerParams(vmem_limit_bytes=vmem * 1024 * 1024),
        cost_estimate=pl.CostEstimate(flops=cost, bytes_accessed=cost, transcendentals=0),
    )(*ins)


def pick(flag, a, b):
    return jnp.where(flag, a, b)


def factor_line(load, count, first, last, inv, ratio, left, right):
    for group, scale in enumerate(SCALES):
        here = load(0)
        excess = 1.0 + pick(first, scale * here, 0.0)
        column = None
        columns = []
        for i in range(count):
            if i < count - 1:
                beyond = load(i + 1)
                face = (0.5 * scale) * (here + beyond)
                inverse = 1.0 / (excess + face)
                portion = face * inverse
                ratio[group, i] = portion
                inv[group, i] = inverse
                columns.append(column)
                column = portion if column is None else column * portion
                excess = 1.0 + portion * excess
                here = beyond
            else:
                excess = excess + pick(last, scale * here, 0.0)
                inverse = 1.0 / excess
                inv[group, i] = inverse
                ratio[group, i] = inverse
                columns.append(column)
        response = inverse
        onward = column * inverse
        right[group, count - 1] = response
        left[group, count - 1] = onward
        for i in range(count - 2, -1, -1):
            portion = ratio[group, i]
            response = portion * response
            start = inv[group, i] if i == 0 else columns[i] * inv[group, i]
            onward = start + portion * onward
            right[group, i] = response
            left[group, i] = onward


def coef_rows(left, right, out, count):
    for group in range(2):
        out[group] = left[group, 0]
        out[2 + group] = left[group, count - 1]
        out[4 + group] = right[group, count - 1]


def pack_kernel(flow, visc, x_odd, y_even, y_odd, cells, sems):
    nx, ny = flow.shape[1], flow.shape[2]
    x_par = lax.rem(lax.axis_index("gx"), 2)
    y_par = lax.rem(lax.axis_index("gy"), 2)
    copies = (
        (flow.at[:, x_par * (nx - 1)], x_odd),
        (flow.at[:, :, (1 - y_par) * (ny - 1)], y_even),
        (flow.at[:, :, y_par * (ny - 1)], y_odd),
        (visc, cells),
    )
    started = [pltpu.make_async_copy(a, b, sems.at[i]) for i, (a, b) in enumerate(copies)]
    for copy in started:
        copy.start()
    for copy in started:
        copy.wait()


def factor_x_kernel(visc, flow, after, ivx, rx, cx, wx, coef_x, x_even):
    nx = visc.shape[0]
    ix = lax.axis_index("gx")
    factor_line(lambda i: visc[i], nx, ix == 0, ix == lax.axis_size("gx") - 1, ivx, rx, cx, wx)
    coef_rows(cx, wx, coef_x, nx)
    coef_x[6] = visc[0]
    coef_x[7] = visc[nx - 1]
    for c in range(4):
        facing = pick(lax.rem(ix, 2) == 0, flow[c, nx - 1], flow[c, 0])
        if c < EARLY:
            coef_x[8 + c] = facing
        x_even[c] = facing


def factor_y_kernel(visc, ivy, ry, cy, wy, coef_y):
    nx, ny, nz = visc.shape
    iy = lax.axis_index("gy")
    rows = visc.reshape(nx * ny, nz)

    def row_y(j):
        return rows[pl.ds(j, nx, stride=ny), :]

    factor_line(row_y, ny, iy == 0, iy == lax.axis_size("gy") - 1, ivy, ry, cy, wy)
    coef_rows(cy, wy, coef_y, ny)
    coef_y[6] = row_y(0)
    coef_y[7] = row_y(ny - 1)


def source_kernel(flow, cx, wx, source, message):
    _, nx, ny, nz = flow.shape
    row = lax.broadcasted_iota(jnp.int32, (ny, nz), 0)
    left = [None] * 4
    right = [None] * 4
    for i in range(nx):
        velocity = [ADVECT * 0.5 * flow[c, i] for c in range(3)]
        for c in range(4):
            f = flow[c, i]
            down = 0.0 if i == 0 else flow[c, i - 1]
            up = 0.0 if i == nx - 1 else flow[c, i + 1]
            below = pick(row == 0, 0.0, pltpu.roll(f, 1, 0))
            above = pick(row == ny - 1, 0.0, pltpu.roll(f, ny - 1, 0))
            z_low = pltpu.roll(f, 1, 1)
            z_high = pltpu.roll(f, nz - 1, 1)
            s = f - (
                velocity[0] * (up - down)
                + velocity[1] * (above - below)
                + velocity[2] * (z_high - z_low)
            )
            if c == 2:
                s = s + BUOYANT * flow[3, i]
            source[c, i] = s
            group = GROUPS[c]
            a, b = cx[group, i] * s, wx[group, i] * s
            left[c] = a if i == 0 else left[c] + a
            right[c] = b if i == 0 else right[c] + b
    for c in range(4):
        message[c] = left[c]
        message[4 + c] = right[c]


def edge_kernel(partial, x_edge_even, x_edge, y_edge_even, y_edge_odd, x_odd, y_even, y_odd, cx, wx, after, message, gap_x, gap_y):
    _, nx, ny, nz = cx.shape
    ix, iy = lax.axis_index("gx"), lax.axis_index("gy")
    x_par, y_par = lax.rem(ix, 2) == 0, lax.rem(iy, 2) == 0
    x_none = (ix == 0) | (ix == lax.axis_size("gx") - 1)
    y_first, y_last = iy == 0, iy == lax.axis_size("gy") - 1
    half = 0.5 * ADVECT
    own_low = half * pick(y_par, y_edge_odd[1], y_edge_even[1])
    own_high = half * pick(y_par, y_edge_even[1], y_edge_odd[1])
    own_x = half * x_edge[0]
    message[pl.ds(8, 4 - EARLY)] = x_edge_even[pl.ds(EARLY, 4 - EARLY)]
    for c in range(4):
        group = GROUPS[c]
        low = own_low * pick(y_par, y_odd[c], y_even[c])
        high = -own_high * pick(y_par, y_even[c], y_odd[c])
        low = pick(y_first, 0.0, low)
        high = pick(y_last, 0.0, high)
        gap_y[c] = low
        gap_y[4 + c] = high
        across = own_x * x_odd[c]
        across = pick(x_none, 0.0, pick(x_par, across, -across))
        gap_x[c] = across
        for k, part in ((c, cx), (4 + c, wx)):
            edge = pick(x_par, part[group, 0], part[group, nx - 1])
            message[k] = partial[k] + edge * across
            rows = part.at[group].reshape(nx * ny, nz)
            for j, gap in ((0, low), (ny - 1, high)):
                line = jnp.sum(rows[pl.ds(j, nx, stride=ny), :] * gap, axis=0, keepdims=True)
                message[k, pl.ds(j, 1)] = message[k, pl.ds(j, 1)] + line


def coef_part(axis, bit, last, mine, theirs, union, weights):
    is_left = (lax.axis_index(axis) & bit) == 0
    next_left = (lax.axis_index(axis) & (2 * bit)) == 0

    def a(k):
        return pick(is_left, mine[k], theirs[k])

    def b(k):
        return pick(is_left, theirs[k], mine[k])

    face = 0.5 * (a(7) + b(6))
    for group, scale in enumerate(SCALES):
        a_lr, b_lr = a(2 + group), b(2 + group)
        m = 1.0 / (1.0 / (scale * face) + a(4 + group) + b(group))
        pa, pb = m * a_lr, m * b_lr
        weights[group] = m
        weights[2 + group] = pa
        weights[4 + group] = pb
        out_ll = a(group) - a_lr * pa
        out_rr = b(4 + group) - b_lr * pb
        if last:
            union[group] = pick(next_left, out_rr, out_ll)
        else:
            union[group] = out_ll
            union[2 + group] = a_lr * pb
            union[4 + group] = out_rr
    if last:
        union[2] = pick(next_left, b(7), a(6))
    else:
        union[6] = a(6)
        union[7] = b(7)


def row_part(axis, bit, last, mine, theirs, weights, union, saved, edged=None):
    is_left = (lax.axis_index(axis) & bit) == 0
    next_left = (lax.axis_index(axis) & (2 * bit)) == 0

    def sides(x, y):
        return pick(is_left, x, y), pick(is_left, y, x)

    for c in range(4):
        group = GROUPS[c]
        a_l, b_l = sides(mine[c], theirs[c])
        a_r, b_r = sides(mine[4 + c], theirs[4 + c])
        if edged is not None:
            coef_mine, coef_theirs, missing = edged
            k = 8 + c if c < EARLY else 8 + c - EARLY
            facing_mine, facing_theirs = (coef_mine, coef_theirs) if c < EARLY else (mine, theirs)
            here = (ADVECT * 0.5) * coef_mine[8] * facing_theirs[k]
            there = (ADVECT * 0.5) * coef_theirs[8] * facing_mine[k]
            missing[c] = here
            a_gap, b_gap = sides(here, there)
            ll = pick(is_left, coef_theirs[group], coef_mine[group])
            rr = pick(is_left, coef_mine[4 + group], coef_theirs[4 + group])
            a_lr, b_lr = sides(coef_mine[2 + group], coef_theirs[2 + group])
            a_l = a_l - a_lr * a_gap
            a_r = a_r - rr * a_gap
            b_l = b_l + ll * b_gap
            b_r = b_r + b_lr * b_gap
        d = b_l - a_r
        saved[c] = weights[group] * d
        out_l = a_l + weights[2 + group] * d
        out_r = b_r - weights[4 + group] * d
        if last:
            union[c] = pick(next_left, out_r, out_l)
        else:
            union[c] = out_l
            union[4 + c] = out_r


def coef_kernel(axis, bit, last, waits, mine, theirs, *refs):
    union, weights = refs[waits:]
    coef_part(axis, bit, last, mine, theirs, union, weights)
    if last:
        union[3] = union[2]


def merge_kernel(axis, bit, last, edged, *refs):
    if edged:
        mine, theirs, weights, coef_mine, coef_theirs, union, saved, missing = refs
        edge = (coef_mine, coef_theirs, missing)
    else:
        mine, theirs, weights, union, saved = refs
        edge = None
    row_part(axis, bit, last, mine, theirs, weights, union, saved, edge)


def last_coef_kernel(mine, theirs, *refs):
    weight = refs[-1]
    face = 0.5 * (mine[2] + theirs[2])
    for group, scale in enumerate(SCALES):
        weight[group] = 1.0 / (1.0 / (scale * face) + mine[group] + theirs[group])


def fluxes(axis, mine, theirs, weight, saved, missing=None):
    index = lax.axis_index(axis)
    bit = lax.axis_size(axis) // 2
    is_left = (index & bit) == 0
    result = []
    for c in range(4):
        group = GROUPS[c]
        d = theirs[c] - mine[c]
        flux = weight[group] * pick(is_left, d, -d)
        zero = jnp.zeros_like(flux)
        low = pick(is_left, zero, flux)
        high = pick(is_left, flux, zero)
        this = bit
        for part, weights in saved[::-1]:
            this = this // 2
            flux = part[c] + weights[4 + group] * high + weights[2 + group] * low
            if this == 1 and missing is not None:
                flux = flux - missing[c]
            side = (index & this) == 0
            low, high = pick(side, low, flux), pick(side, flux, high)
        result.append((low, high))
    return result


def local_kernel(source, gap_x, gap_y, ivx, rx, cx, wx, local_t, cx_t, wx_t, scratch):
    _, nx, ny, nz = source.shape
    x_par = lax.rem(lax.axis_index("gx"), 2) == 0
    row = lax.broadcasted_iota(jnp.int32, (ny, nz), 0)

    def right_side(c, i):
        s = source[c, i]
        s = s + pick(row == 0, gap_y[c, pl.ds(i, 1)], 0.0)
        s = s + pick(row == ny - 1, gap_y[4 + c, pl.ds(i, 1)], 0.0)
        if i == 0:
            s = s + pick(x_par, gap_x[c], 0.0)
        if i == nx - 1:
            s = s + pick(x_par, 0.0, gap_x[c])
        return s

    for c in range(4):
        group = GROUPS[c]
        running = right_side(c, 0)
        forward = [running]
        for i in range(1, nx):
            running = right_side(c, i) + rx[group, i - 1] * running
            forward.append(running)
        value = running * ivx[group, nx - 1]
        scratch[c, pl.ds((nx - 1) * ny, ny)] = value
        for i in range(nx - 2, -1, -1):
            value = forward[i] * ivx[group, i] + rx[group, i] * value
            scratch[c, pl.ds(i * ny, ny)] = value
        for j in range(ny):
            local_t[c, j] = scratch[c, pl.ds(j, nx, stride=ny), :]
    for group in range(2):
        c_rows = cx.at[group].reshape(nx * ny, nz)
        w_rows = wx.at[group].reshape(nx * ny, nz)
        for j in range(ny):
            cx_t[group, j] = c_rows[pl.ds(j, nx, stride=ny), :]
            wx_t[group, j] = w_rows[pl.ds(j, nx, stride=ny), :]


def y_start_kernel(stages, *refs):
    mine, theirs, weight, missing = refs[:4]
    parts = refs[4 : 4 + 2 * stages]
    local_t, cx_t, wx_t, cy, wy, solved, message, flux_low, flux_high = refs[4 + 2 * stages :]
    _, ny, nx, nz = local_t.shape
    saved = list(zip(parts[::2], parts[1::2]))
    for c, (low, high) in enumerate(fluxes("gx", mine, theirs, weight, saved, missing)):
        flux_low[c] = low
        flux_high[c] = high
    for c in range(4):
        group = GROUPS[c]
        left = right = None
        for j in range(ny):
            low = flux_low[c, pl.ds(j, 1)]
            high = flux_high[c, pl.ds(j, 1)]
            value = local_t[c, j] + (wx_t[group, j] * high - cx_t[group, j] * low)
            solved[c, j] = value
            a, b = cy[group, j] * value, wy[group, j] * value
            left = a if j == 0 else left + a
            right = b if j == 0 else right + b
        message[c] = left
        message[4 + c] = right


def y_local_kernel(solved, ivy, ry, cy, wy, local, cy_t, wy_t):
    _, ny, nx, nz = solved.shape
    for part, turned in ((cy, cy_t), (wy, wy_t)):
        for group in range(2):
            out = turned.at[group].reshape(nx * ny, nz)
            for j in range(ny):
                out[pl.ds(j, nx, stride=ny), :] = part[group, j]
    for c in range(4):
        group = GROUPS[c]
        rows = local.at[c].reshape(nx * ny, nz)
        running = solved[c, 0]
        forward = [running]
        for j in range(1, ny):
            running = solved[c, j] + ry[group, j - 1] * running
            forward.append(running)
        value = running * ivy[group, ny - 1]
        rows[pl.ds(ny - 1, nx, stride=ny), :] = value
        for j in range(ny - 2, -1, -1):
            value = forward[j] * ivy[group, j] + ry[group, j] * value
            rows[pl.ds(j, nx, stride=ny), :] = value


def finish_kernel(stages, *refs):
    mine, theirs, weight = refs[:3]
    parts = refs[3 : 3 + 2 * stages]
    local, cy_t, wy_t, out, buffer, flux_low, flux_high, sems = refs[3 + 2 * stages :]
    saved = list(zip(parts[::2], parts[1::2]))
    nx = local.shape[1]
    for c, (low, high) in enumerate(fluxes("gy", mine, theirs, weight, saved)):
        flux_low[c] = low
        flux_high[c] = high
    copies = []
    for c in range(4):
        group = GROUPS[c]
        for i in range(nx):
            low = flux_low[c, pl.ds(i, 1)]
            high = flux_high[c, pl.ds(i, 1)]
            buffer[c, i] = local[c, i] + (wy_t[group, i] * high - cy_t[group, i] * low)
        copies.append(pltpu.make_async_copy(buffer.at[c], out.at[c], sems.at[c]))
        copies[-1].start()
    for copy in copies:
        copy.wait()


def swap(array, axis, bit):
    return lax.ppermute(array, axis, [(i, i ^ bit) for i in range(lax.axis_size(axis))])


def after_all(spec_count, waits=1):
    return [VMEM] * spec_count + [pl.BlockSpec(memory_space=pl.ANY)] * waits


def merge_coefs(axis, bit, mine, theirs, after=()):
    last = 4 * bit == lax.axis_size(axis)
    shape = mine.shape[1:]
    return call(
        functools.partial(coef_kernel, axis, bit, last, len(after)),
        (mine, theirs, *after),
        [(4 if last else 8,) + shape, (6,) + shape],
        in_specs=after_all(2, len(after)),
    )


def merge_rows(axis, bit, mine, theirs, weights, coefs=()):
    last = 4 * bit == lax.axis_size(axis)
    shape = mine.shape[1:]
    return call(
        functools.partial(merge_kernel, axis, bit, last, bool(coefs)),
        (mine, theirs, weights, *coefs),
        [(4 if last else 8,) + shape, (4,) + shape] + [(4,) + shape] * bool(coefs),
    )


def per_device(flow, visc):
    fields, nx, ny, nz = flow.shape
    mx, my = lax.axis_size("gx"), lax.axis_size("gy")
    along_x, along_y = (2, nx, ny, nz), (2, ny, nx, nz)
    along_x, along_y = (2, nx, ny, nz), (2, ny, nx, nz)
    x_edge, y_edge_even, y_edge_odd, cells = call(
        pack_kernel,
        tuple(pltpu.with_memory_space_constraint(array, pltpu.HBM) for array in (flow, visc)),
        [(fields, ny, nz)] + [(fields, nx, nz)] * 2 + [(nx, ny, nz)],
        scratch=[pltpu.SemaphoreType.DMA((4,))],
        in_specs=[HBM, HBM],
    )
    pairs = []
    for i in range(mx):
        for j in range(my):
            inner = 0 < i < mx - 1
            partner = ((i - 1 ^ 1) + 1, j) if inner else (i, j ^ 1)
            pairs.append((i * my + j, partner[0] * my + partner[1]))
    x_odd = lax.ppermute(x_edge, ("gx", "gy"), pairs)
    y_odd = lax.ppermute(
        y_edge_odd, "gy", [(i, (i - 1 ^ 1) + 1) if 0 < i < my - 1 else (i, my - 1 - i) for i in range(my)]
    )
    y_even = swap(y_edge_even, "gy", 1)
    ivx, rx, cx, wx, coef_x, x_edge_even = call(
        factor_x_kernel,
        (cells, flow, y_even),
        [along_x] * 4 + [(8 + EARLY, ny, nz), (fields, ny, nz)],
        in_specs=after_all(2),
    )

    ivy, ry, cy, wy, coef_y = call(factor_y_kernel, (cells,), [along_y] * 4 + [(8, nx, nz)])
    coef_x_theirs = swap(coef_x, "gx", 1)
    source, partial = call(source_kernel, (flow, cx, wx), [(fields, nx, ny, nz), (8, ny, nz)])
    message, gap_x, gap_y = call(
        edge_kernel,
        (partial, x_edge_even, x_edge, y_edge_even, y_edge_odd, x_odd, y_even, y_odd, cx, wx, ivy),
        [(12 - EARLY, ny, nz), (fields, ny, nz), (2 * fields, nx, nz)],
        in_specs=after_all(10),
    )
    local_t, cx_t, wx_t = call(
        local_kernel,
        (source, gap_x, gap_y, ivx, rx, cx, wx),
        outs=[(fields, ny, nx, nz), along_y, along_y],
        scratch=[pltpu.VMEM((fields, nx * ny, nz), F32)],
        cost=1000,
    )

    y_coefs, y_coefs_theirs, y_weights = coef_y, swap(coef_y, "gy", 1), []
    bit = 1
    while 2 * bit < my:
        y_coefs, weights = merge_coefs("gy", bit, y_coefs, y_coefs_theirs)
        y_weights.append(weights)
        y_coefs_theirs = swap(y_coefs, "gy", 2 * bit)
        bit *= 2

    saved = []
    coefs, coefs_theirs, rows = coef_x, coef_x_theirs, message
    bit = 1
    while 2 * bit < mx:
        rows_theirs = swap(rows, "gx", bit)
        after = (local_t, y_weights[0]) if bit == 1 else (rows,)
        merged, weights = merge_coefs("gx", bit, coefs, coefs_theirs, after)
        merged_theirs = swap(merged, "gx", 2 * bit)
        extra = (coefs, coefs_theirs) if bit == 1 else ()
        rows, part, *gap = merge_rows("gx", bit, rows, rows_theirs, weights, extra)
        if gap:
            missing = gap[0]
        saved += [part, weights]
        coefs, coefs_theirs = merged, merged_theirs
        bit *= 2
    rows_theirs = swap(rows, "gx", bit)
    (weight,) = call(last_coef_kernel, (coefs, coefs_theirs), [(2, ny, nz)])

    solved, rows = call(
        functools.partial(y_start_kernel, len(saved) // 2),
        (rows, rows_theirs, weight, missing, *saved, local_t, cx_t, wx_t, cy, wy),
        [(fields, ny, nx, nz), (8, nx, nz)],
        scratch=[pltpu.VMEM((fields, ny, nz), F32)] * 2,
    )
    local_y, cy_t, wy_t = call(
        y_local_kernel, (solved, ivy, ry, cy, wy), [(fields, nx, ny, nz), along_x, along_x]
    )
    (y_weight,) = call(
        last_coef_kernel, (y_coefs, y_coefs_theirs, local_y), [(2, nx, nz)], in_specs=after_all(2)
    )
    saved = []
    for step, weights in enumerate(y_weights):
        bit = 1 << step
        rows, part = merge_rows("gy", bit, rows, swap(rows, "gy", bit), weights)
        saved += [part, weights]
    rows_theirs = swap(rows, "gy", my // 2)
    (out,) = call(
        functools.partial(finish_kernel, len(saved) // 2),
        (rows, rows_theirs, y_weight, *saved, local_y, cy_t, wy_t),
        [(fields, nx, ny, nz)],
        scratch=[
            pltpu.VMEM((fields, nx, ny, nz), F32),
            pltpu.VMEM((fields, nx, nz), F32),
            pltpu.VMEM((fields, nx, nz), F32),
            pltpu.SemaphoreType.DMA((fields,)),
        ],
        out_specs=[HBM],
    )
    return out


def solution(mesh):
    placed = (P(None, "gx", "gy", None), P("gx", "gy", None))
    return jax.shard_map(
        per_device, mesh=mesh, in_specs=placed, out_specs=P(None, "gx", "gy", None), check_vma=False
    )
```
